32 devices in a mesh: dp: 8 (over y, x, core), bag: 4 (over z).
Axes of the slice: x: 2, y: 2, z: 4, core: 2. Of those that a mesh axis runs over, the one named last changes fastest.
Arguments:
- home_tokens: bfloat16 [4096, 3072], P('dp', 'bag'), may hold values from -6 to 6
- mod_weight: bfloat16 [2, 3072, 3072], P(None, None, 'bag'), may hold values from -0.109375 to 0.109375
- qkv_weight: bfloat16 [3, 3072, 3072], P(None, None, 'bag')
- norm_gain: float32 [2, 3072], P(None, 'bag'), may hold values from 0.5 to 8
- output_weight: bfloat16 [3072, 3072], P('bag'), may hold values from -0.109375 to 0.109375
- row_plan: int32 [4096], replicated, may hold values from 0 to 5119, as said below
- sample_lengths: int32 [8, 4], replicated, may hold values from 0 to 640, as said below
- modality: int32 [8, 4], replicated, may hold values from 0 to 1
Outputs:
- block_output: bfloat16 [4096, 3072], P('dp', 'bag')
The draws below stay inside these ranges and needn't reach their ends.
Inputs may be any that keep to these rules, and one draw needn't show every extreme that they name: `row_plan`: row r sits on home r // 512; no two rows share a value; the rows of bag j fill exactly its slots 0 to sample_ends[j, 3] - 1; no home sends more than 128 rows to one bag, and some home sends exactly 128 rows to some bag. `sample_lengths`: row j lists the lengths of the samples of bag j in slot order, zeros allowed; each row sums to at most 640, and some bag holds one sample of 640 tokens.
All inputs are finite; a program needn't handle non-finite values.
Results may differ from the reference program's by a relative error of at most 0.013.
The reference program's roundings to bfloat16 on the way count: a program that leaves them out, or rounds other values in their place, can miss the bound.
Values may be sent and summed in bfloat16 or wider, within the bound.
No kernel may reach another device: no remote copies, remote signals or barrier semaphores. Data moves between devices by JAX's collectives and lax.ppermute only.
A program may use at most 192 MiB of HBM per device.

```python
import math
import jax
import jax.numpy as jnp
from jax import lax

D = 3072
H = 48
HD = 64
SEGS = 4
HOME = 512
PACK = 640
TOTAL = 4096
N_DP = 8
N_BAG = 4


def packing(key):
    folded = jax.random.fold_in(key, 7001)
    subkeys = jax.random.split(folded, 7)
    unit_rows = HOME // N_DP
    half_unit = unit_rows // 2
    pair_count = N_DP // 2
    bag_order = jax.random.permutation(subkeys[0], N_DP)
    home_orders = jax.vmap(lambda subkey: jax.random.permutation(subkey, N_DP))(jax.random.split(subkeys[1], pair_count))
    home_ranks = jnp.argsort(home_orders, axis=1)
    tilt_signs = jax.random.randint(subkeys[2], (pair_count, N_DP), -1, 2)
    tilt_signs = tilt_signs.at[0].set(1)
    chosen = (home_ranks < N_DP // 2).astype(jnp.int32)
    tilt_rows = tilt_signs * chosen
    spare_rows = jax.random.randint(subkeys[3], (pair_count, N_DP), 0, half_unit + 1)
    leader = home_orders[0, 0]
    spare_rows = spare_rows.at[0, leader].set(half_unit).at[0, (leader + 1) % N_DP].set(0)
    swing_rows = half_unit * tilt_rows + spare_rows - jnp.roll(spare_rows, -1, axis=1)
    counts = jnp.zeros((N_DP, N_DP), jnp.int32)
    counts = counts.at[:, bag_order[0::2]].set((unit_rows + swing_rows).T)
    counts = counts.at[:, bag_order[1::2]].set((unit_rows - swing_rows).T)
    bag_fills = jnp.sum(counts, axis=0)
    inclusive = jnp.cumsum(counts, axis=1)
    ahead_rows = jnp.cumsum(counts, axis=0) - counts
    row_ids = jnp.arange(HOME, dtype=jnp.int32)
    row_bag = jnp.sum((row_ids[None, :, None] >= inclusive[:, None, :]).astype(jnp.int32), axis=2)
    run_begin = jnp.take_along_axis(inclusive - counts, row_bag, axis=1)
    within = row_ids[None, :] - run_begin
    incoming = jnp.take_along_axis(ahead_rows, row_bag, axis=1) + within
    slot_ids = jnp.arange(PACK, dtype=jnp.int32)[None, :]
    slot_keys = jax.random.randint(subkeys[4], (N_DP, PACK), 0, 2 ** 16) * PACK + slot_ids
    slot_keys = slot_keys + (slot_ids >= bag_fills[:, None]).astype(jnp.int32) * 2 ** 29
    slot_order = jnp.argsort(slot_keys, axis=1).astype(jnp.int32)
    row_slot = slot_order[row_bag, incoming]
    row_value = row_bag * PACK + row_slot
    shuffle = jax.vmap(lambda subkey: jax.random.permutation(subkey, HOME))(jax.random.split(subkeys[5], N_DP))
    plan_rows = jax.vmap(lambda values_in, shuffle_order: jnp.zeros((HOME,), jnp.int32).at[shuffle_order].set(values_in))(row_value, shuffle)
    plan_rows = plan_rows.reshape(N_DP * HOME).astype(jnp.int32)
    cut_points = jax.random.randint(subkeys[6], (N_DP, SEGS - 1), 1, jnp.maximum(bag_fills, 2)[:, None])
    is_full = jnp.arange(N_DP) == bag_order[0]
    cut_points = jnp.where(is_full[:, None], bag_fills[:, None], cut_points)
    cut_points = jnp.sort(cut_points, axis=1)
    bounds = jnp.concatenate([jnp.zeros((N_DP, 1), jnp.int32), cut_points.astype(jnp.int32), bag_fills[:, None].astype(jnp.int32)], axis=1)
    length_list = (bounds[:, 1:] - bounds[:, :-1]).astype(jnp.int32)
    return (plan_rows, length_list)


def draw_row_plan(key, part):
    return packing(key)[0]


def draw_sample_lengths(key, part):
    return packing(key)[1]


def draw_qkv_weight(key, part):
    folded = jax.random.fold_in(key, 7101)
    normals = jnp.clip(jax.random.normal(folded, (3, D, H * HD), jnp.float32), -4.0, 4.0) * D ** (-0.5)
    return normals.astype(jnp.bfloat16)


def draw_norm_gain(key, part):
    folded = jax.random.fold_in(key, 7201)
    subkeys = jax.random.split(folded, 1)
    element = jnp.exp(jax.random.uniform(subkeys[0], (2, H * HD), jnp.float32, 0.0, math.log(3.0)))
    return element


def place_ends(array, own_key, smallest, top_value):
    index_at = [jax.random.randint(jax.random.fold_in(own_key, axis), (), 0, length) for axis, length in enumerate(array.shape)]
    widest = array.shape.index(max(array.shape))
    beside = index_at[:widest] + [(index_at[widest] + 1) % array.shape[widest]] + index_at[widest + 1:]
    return array.at[tuple(index_at)].set(smallest).at[tuple(beside)].set(top_value)


def steps_of(key, shape, pieces, smallest, high):
    def one(position, parts):
        heights = jax.random.uniform(jax.random.fold_in(jax.random.fold_in(key, 6), position), (parts,), jnp.float32, smallest / len(pieces), high / len(pieces))
        return jnp.repeat(jnp.exp(heights), shape[position] // parts).reshape((-1,) + (1,) * (len(shape) - position - 1))

    loudness = one(*pieces[0])
    for cut in pieces[1:]:
        loudness = loudness * one(*cut)
    return loudness


def scatter_about(rng, shape, scale, reach, cuts=(), held_as=jnp.bfloat16):
    entries = scale * jax.random.normal(rng, shape, jnp.float32)
    if cuts:
        entries = entries * steps_of(rng, shape, cuts, -0.22, 0.18)
    return jnp.clip(entries, -reach, reach).astype(held_as)


def setup_inputs(seed: int = 0) -> dict:
    splits = jax.random.split(jax.random.key(seed), 9)
    return {
        "home_tokens": scatter_about(splits[0], (TOTAL, D), 1.0, 6.0, ((0, 8), (1, 4))),
        "mod_weight": scatter_about(splits[1], (2, D, D), D ** -0.5, 0.109375, ((2, 4),)),
        "qkv_weight": draw_qkv_weight(jax.random.fold_in(splits[8], 71), 0),
        "norm_gain": draw_norm_gain(jax.random.fold_in(splits[8], 71), 0),
        "output_weight": scatter_about(splits[4], (H * HD, D), (H * HD) ** -0.5, 0.109375, ((0, 4),)),
        "row_plan": draw_row_plan(jax.random.fold_in(splits[8], 71), 0),
        "sample_lengths": draw_sample_lengths(jax.random.fold_in(splits[8], 71), 0),
        "modality": place_ends(jax.random.randint(splits[7], (N_DP, SEGS), 0, 2), jax.random.fold_in(splits[7], 1), 0, 1).astype(jnp.int32),
    }


epsilon = 1e-06

def head_norm(heads_in, gains):
    centre = lax.optimization_barrier(jnp.mean(heads_in, axis=-1, keepdims=True))
    shifted = heads_in - centre
    spread = lax.optimization_barrier(jnp.mean(shifted * shifted, axis=-1, keepdims=True))
    return shifted * lax.rsqrt(spread + epsilon) * gains

def reference(home_tokens, mod_weight, qkv_weight, norm_gain, output_weight, row_plan, sample_lengths, modality):
    sample_ends = jnp.cumsum(sample_lengths, axis=1).astype(jnp.int32)
    bag_of = (row_plan // PACK).astype(jnp.int32)
    slot_of = (row_plan % PACK).astype(jnp.int32)
    row_ends = sample_ends[bag_of]
    row_sample = lax.optimization_barrier(jnp.sum((slot_of[:, None] >= row_ends).astype(jnp.int32), axis=1))
    row_modality = modality[bag_of, row_sample]
    leading_product = jnp.dot(home_tokens, mod_weight[0], preferred_element_type=jnp.float32)
    second_product = jnp.dot(home_tokens, mod_weight[1], preferred_element_type=jnp.float32)
    projected = jnp.where(row_modality[:, None] == 0, leading_product, second_product).astype(jnp.bfloat16)
    packed = jnp.zeros((N_DP * PACK, D), jnp.bfloat16).at[row_plan].set(projected)
    group_heads = H // N_BAG
    group_width = group_heads * HD
    slot_ids = jnp.arange(PACK, dtype=jnp.int32)

    def one_bag(bag_index):
        bag_rows = lax.dynamic_slice_in_dim(packed, (bag_index * PACK).astype(jnp.int32), PACK, 0)
        bag_ends = lax.dynamic_index_in_dim(sample_ends, bag_index, 0, keepdims=False)
        sample_ids = lax.optimization_barrier(jnp.sum((slot_ids[:, None] >= bag_ends[None, :]).astype(jnp.int32), axis=1))
        allowed = sample_ids[:, None] == sample_ids[None, :]

        def one_group(group_index):
            offset = (group_index * group_width).astype(jnp.int32)
            weights = lax.dynamic_slice_in_dim(qkv_weight, offset, group_width, 2)
            gains = lax.dynamic_slice_in_dim(norm_gain, offset, group_width, 1)
            queries = jnp.dot(bag_rows, weights[0], preferred_element_type=jnp.float32)
            keys_raw = jnp.dot(bag_rows, weights[1], preferred_element_type=jnp.float32)
            values = jnp.dot(bag_rows, weights[2], preferred_element_type=jnp.float32)
            queries = head_norm(queries.reshape(PACK, group_heads, HD), gains[0].reshape(group_heads, HD)).astype(jnp.bfloat16)
            keys_normed = head_norm(keys_raw.reshape(PACK, group_heads, HD), gains[1].reshape(group_heads, HD)).astype(jnp.bfloat16)
            values = values.astype(jnp.bfloat16).reshape(PACK, group_heads, HD)
            scores = jnp.einsum('qhd,khd->hqk', queries.astype(jnp.float32), keys_normed.astype(jnp.float32)) * HD ** (-0.5)
            scores = jnp.where(allowed[None], scores, -jnp.inf)
            row_max = lax.optimization_barrier(jnp.max(scores, axis=2, keepdims=True))
            raised = jnp.exp(scores - row_max)
            weights_soft = (raised / lax.optimization_barrier(jnp.sum(raised, axis=2, keepdims=True))).astype(jnp.bfloat16)
            attended = jnp.einsum('hqk,khd->qhd', weights_soft.astype(jnp.float32), values.astype(jnp.float32))
            attended = attended.astype(jnp.bfloat16).reshape(PACK, group_width)
            out_rows = lax.dynamic_slice_in_dim(output_weight, offset, group_width, 0)
            partial_value = jnp.dot(attended, out_rows, preferred_element_type=jnp.float32).astype(jnp.bfloat16)
            return lax.optimization_barrier(partial_value).astype(jnp.float32)
        return lax.optimization_barrier(jnp.sum(lax.map(one_group, jnp.arange(N_BAG, dtype=jnp.int32)), axis=0))
    summed = lax.map(one_bag, jnp.arange(N_DP, dtype=jnp.int32)).reshape(N_DP * PACK, D)
    return summed[row_plan].astype(jnp.bfloat16)
```

```python
import functools

import jax
import jax.numpy as jnp
from jax import lax
from jax.experimental import pallas as pl
from jax.experimental.pallas import tpu as pltpu
from jax.sharding import PartitionSpec as P

HD = 64
EPSILON = 1e-06
VMEM_LIMIT = 56 * 1024 * 1024
BF16 = jnp.bfloat16
F32 = jnp.float32


def params():
    return pltpu.CompilerParams(vmem_limit_bytes=VMEM_LIMIT)


def up16(count):
    return (count + 15) // 16 * 16


def iota(shape, dim):
    return lax.broadcasted_iota(jnp.int32, shape, dim)


def dot(left, right):
    return jnp.dot(left, right, preferred_element_type=F32)


def dot_nt(left, right):
    return lax.dot_general(left, right, (((1,), (1,)), ((), ())), preferred_element_type=F32)


def total(mask, axis):
    return jnp.sum(jnp.where(mask, 1.0, 0.0), axis=axis, keepdims=True).astype(jnp.int32)


def bag_numbers(plan, bags, pack):
    number = jnp.zeros_like(plan)
    for bag in range(1, bags):
        number += (plan >= bag * pack).astype(jnp.int32)
    return number


def order_kernel(bags, pack, plan_col, plan_row, tokens, even, odd, order_even, order_odd, where_row, where_col):
    count = plan_row.shape[1]
    bag_col = bag_numbers(plan_col[...], bags, pack)
    bag_row = bag_numbers(plan_row[...], bags, pack)
    same = bag_col == bag_row
    above = iota((count, count), 0) < iota((count, count), 1)
    below = iota((count, count), 0) > iota((count, count), 1)
    place_col = total(same & below, 1)
    place_row = total(same & above, 0)
    part_col = place_col & 1
    part_row = place_row & 1
    for part, (ordered, order) in enumerate(((even, order_even), (odd, order_odd))):
        rank_row = total(above & (part_col == part), 0)
        rows = ordered.shape[0]
        onehot = ((iota((rows, count), 0) == rank_row) & (part_row == part)).astype(F32).astype(BF16)
        order[...] = onehot
        ordered[...] = dot(onehot, tokens[...]).astype(BF16)
    where_row[...] = bag_row * 65536 + place_row
    where_col[...] = bag_col * 65536 + place_col


def send_kernel(bags, pack, half, ends, modality, plan_row, where_row, where_col, order_even, order_odd,
                send_even, send_odd, kind_even, kind_odd, final):
    count = plan_row.shape[1]
    slots = bags * half
    bag_row = where_row[...] >> 16
    place_row = where_row[...] & 65535
    bag_col = where_col[...] >> 16
    place_col = where_col[...] & 65535
    plan = plan_row[...]
    kind = jnp.zeros((1, count), F32)
    for bag in range(bags):
        begin = bag * pack
        for sample in range(ends.shape[1]):
            end = bag * pack + ends[bag, sample]
            inside = (plan >= begin) & (plan < end)
            kind = jnp.where(inside, modality[bag, sample].astype(F32), kind)
            begin = end
    slot_row = bag_row * half + (place_row >> 1)
    for part, (order, send, kinds) in enumerate(((order_even, send_even, kind_even), (order_odd, send_odd, kind_odd))):
        target = (iota((slots, count), 0) == slot_row) & ((place_row & 1) == part)
        send[...] = dot_nt(target.astype(F32).astype(BF16), order[...]).astype(BF16)
        picked = jnp.sum(order[...].astype(F32) * kind, axis=1, keepdims=True)
        kinds[...] = jnp.broadcast_to(picked, kinds.shape)
    back_col = bag_col * (2 * half) + (place_col & 1) * half + (place_col >> 1)
    final[...] = (iota(final.shape, 1) == back_col).astype(F32).astype(BF16)


def bag_kernel(pack, half, me, ends, plan, pack_even, pack_odd, back, samples, held):
    homes, count = plan.shape
    slot = plan[...] - me[0] * pack
    mine = (slot >= 0) & (slot < pack)
    ahead = (iota((count, count), 0) < iota((count, count), 1)).astype(F32).astype(BF16)
    place = dot(mine.astype(F32).astype(BF16), ahead).astype(jnp.int32)
    place = jnp.where(mine, place, -1)
    filled = total(mine, 1)
    first = 0
    for part, packer in enumerate((pack_even, pack_odd)):
        rows, slots = packer.shape
        lanes = iota((1, slots), 1)
        shift = jnp.zeros((1, slots), jnp.int32)
        limit = jnp.zeros((1, slots), jnp.int32)
        start = jnp.zeros((1, 1), jnp.int32)
        for home in range(homes):
            here = (filled[home:home + 1, :] + (1 - part)) >> 1
            of_home = (lanes >= home * half) & (lanes < (home + 1) * half)
            shift = jnp.where(of_home, start - home * half, shift)
            limit = jnp.where(of_home, here + home * half, limit)
            down = iota((half, back.shape[1]), 0)
            across = iota((half, back.shape[1]), 1)
            block = ((across == down + start + first) & (down < here)).astype(F32).astype(BF16)
            at = (home * 2 + part) * half
            back[at:at + half, :] = block
            chosen = place[home:home + 1, :] == iota((half, count), 0) * 2 + part
            slot_here = jnp.sum(jnp.where(chosen, slot[home:home + 1, :].astype(F32), 0.0), axis=1, keepdims=True)
            slot_here = slot_here.astype(jnp.int32)
            number = jnp.ones((half, 1), jnp.int32)
            for sample in range(ends.shape[1]):
                number += (slot_here >= ends[me[0], sample]).astype(jnp.int32)
            held[home * half:(home + 1) * half, :] = jnp.broadcast_to(number.astype(F32), (half, held.shape[1])).astype(BF16)
            start = start + here
        onehot = ((iota((rows, slots), 0) == lanes + shift) & (lanes < limit)).astype(F32).astype(BF16)
        packer[...] = onehot
        samples[first:first + rows, :] = dot(onehot, held[...])
        first += rows


def project_kernel(rows_in, kinds, weight, send, out):
    rows = rows_in[...]
    image = dot(rows, weight[0])
    video = dot(rows, weight[1])
    projected = jnp.where(kinds[:, :1] == 0.0, image, video).astype(BF16)
    out[...] = dot(send[...], projected).astype(BF16)


def project(rows_in, kinds, weight, send):
    rows, depth = rows_in.shape
    width = weight.shape[2]
    step = 256 if width % 256 == 0 else width
    slots = send.shape[0]
    return pl.pallas_call(
        project_kernel,
        grid=(width // step,),
        in_specs=[
            pl.BlockSpec((rows, depth), lambda i: (0, 0)),
            pl.BlockSpec(kinds.shape, lambda i: (0, 0)),
            pl.BlockSpec((2, depth, step), lambda i: (0, 0, i)),
            pl.BlockSpec(send.shape, lambda i: (0, 0)),
        ],
        out_specs=pl.BlockSpec((slots, step), lambda i: (0, i)),
        out_shape=jax.ShapeDtypeStruct((slots, width), BF16),
        compiler_params=params(),
        cost_estimate=pl.CostEstimate(
            flops=4 * rows * depth * width, bytes_accessed=weight.size * 2, transcendentals=0
        ),
        name="project",
    )(rows_in, kinds, weight, send)


def split_dot(value, square):
    high = value.astype(BF16)
    low = (value - high.astype(F32)).astype(BF16)
    return dot(high, square) + dot(low, square)


def qkv_kernel(rows_in, weight, gain, queries, keys, values):
    rows = rows_in[...]
    step = weight.shape[2]
    square = (iota((step, step), 0) // HD == iota((step, step), 1) // HD).astype(F32) * (1.0 / HD)
    square = square.astype(BF16)
    for index, (out, scale) in enumerate(((queries, HD ** -0.5), (keys, 1.0))):
        raw = dot(rows, weight[index])
        shifted = raw - split_dot(raw, square)
        spread = split_dot(shifted * shifted, square)
        out[...] = (shifted * lax.rsqrt(spread + EPSILON) * gain[index:index + 1, :] * scale).astype(BF16)
    values[...] = dot(rows, weight[2]).astype(BF16)


def make_qkv(rows_in, weight, gain):
    rows, depth = rows_in.shape
    width = weight.shape[2]
    step = 256 if width % 256 == 0 else 128
    part = pl.BlockSpec((rows, step), lambda i: (0, i))
    shape = jax.ShapeDtypeStruct((rows, width), BF16)
    return pl.pallas_call(
        qkv_kernel,
        grid=(width // step,),
        in_specs=[
            pl.BlockSpec((rows, depth), lambda i: (0, 0)),
            pl.BlockSpec((3, depth, step), lambda i: (0, 0, i)),
            pl.BlockSpec((2, step), lambda i: (0, i)),
        ],
        out_specs=[part] * 3,
        out_shape=[shape] * 3,
        compiler_params=params(),
        cost_estimate=pl.CostEstimate(
            flops=6 * rows * depth * width, bytes_accessed=weight.size * 2, transcendentals=0
        ),
        name="qkv",
    )(rows_in, weight, gain)


def attend_kernel(sample_col, sample_row, qa, ka, va, qb, kb, vb, out, bias, keys, values):
    first = qa.shape[0]
    second = qb.shape[0]

    @pl.when(pl.program_id(0) == 0)
    def _():
        bias[...] = jnp.where(sample_col[:, :1] == sample_row[...], 0.0, -1e30)

    keys[:first, :] = ka[...]
    keys[first:, :] = kb[...]
    values[:first, :] = va[...]
    values[first:, :] = vb[...]
    width = qa.shape[1]
    for part, begin, rows in ((qa, 0, first), (qb, first, second)):
        count = 3 if rows % 48 == 0 else 2
        step = rows // count
        for block in range(count):
            low = block * step
            query = part[low:low + step, :]
            lanes = iota((step, width), 1)
            result = jnp.zeros((step, width), F32)
            for head in range(width // HD):
                own = (lanes >= head * HD) & (lanes < (head + 1) * HD)
                masked = jnp.where(own, query, jnp.zeros_like(query))
                scores = dot_nt(masked, keys[...]) + bias[begin + low:begin + low + step, :]
                top = jnp.max(scores, axis=1, keepdims=True)
                raised = jnp.exp(scores - top)
                weight = jnp.sum(raised, axis=1, keepdims=True)
                mixed = dot(raised.astype(BF16), values[...]) / weight
                result = jnp.where(own, mixed, result)
            out[begin + low:begin + low + step, :] = result.astype(BF16)


def attend(sample_col, sample_row, parts_a, parts_b):
    first, width = parts_a[0].shape
    second = parts_b[0].shape[0]
    rows = first + second
    step = 2 * HD
    spec_a = pl.BlockSpec((first, step), lambda i: (0, i))
    spec_b = pl.BlockSpec((second, step), lambda i: (0, i))
    return pl.pallas_call(
        attend_kernel,
        grid=(width // step,),
        in_specs=[
            pl.BlockSpec(sample_col.shape, lambda i: (0, 0)),
            pl.BlockSpec(sample_row.shape, lambda i: (0, 0)),
        ] + [spec_a] * 3 + [spec_b] * 3,
        out_specs=pl.BlockSpec((rows, step), lambda i: (0, i)),
        out_shape=jax.ShapeDtypeStruct((rows, width), BF16),
        scratch_shapes=[
            pltpu.VMEM((rows, rows), F32),
            pltpu.VMEM((rows, step), BF16),
            pltpu.VMEM((rows, step), BF16),
        ],
        compiler_params=params(),
        cost_estimate=pl.CostEstimate(
            flops=4 * rows * rows * width, bytes_accessed=8 * rows * width, transcendentals=rows * rows * width // HD
        ),
        name="attend",
    )(sample_col, sample_row, *parts_a, *parts_b)


def line_sum(partial, width):
    members = lax.axis_size("bag")
    mine = lax.axis_index("bag")

    def piece(index):
        index = jnp.clip(index, 0, members - 1)
        return lax.dynamic_slice_in_dim(partial, index * width, width, 1).astype(F32)

    up = down = None
    for step in range(1, members):
        to_up = piece(members - step + mine)
        to_down = piece(mine + step - members)
        if step > 1:
            to_up = to_up + up.astype(F32)
            to_down = to_down + down.astype(F32)
        up = lax.ppermute(to_up.astype(BF16), "bag", [(i, i + 1) for i in range(step)])
        down = lax.ppermute(to_down.astype(BF16), "bag", [(i, i - 1) for i in range(members - step, members)])
    return (piece(mine) + up.astype(F32) + down.astype(F32)).astype(BF16)


def body(
    home_tokens,
    mod_weight,
    qkv_weight,
    norm_gain,
    output_weight,
    row_plan,
    sample_lengths,
    modality,
):
    bags = lax.axis_size("dp")
    me = lax.axis_index("dp")
    count, width = home_tokens.shape
    pack = count + count // 4
    capacity = 2 * count // bags
    half = capacity // 2
    slots = bags * half
    home_rows = (up16(count // 2 + bags // 2), up16(count // 2))
    bag_rows = (up16(pack // 2 + bags // 2), up16(pack // 2))
    rows = sum(bag_rows)
    vmem = pl.BlockSpec(memory_space=pltpu.VMEM)
    smem = pl.BlockSpec(memory_space=pltpu.SMEM)
    ends = jnp.cumsum(sample_lengths, axis=1)

    own_plan = lax.dynamic_slice_in_dim(row_plan, me * count, count, 0)
    plan_row = own_plan.reshape(1, count)
    plan_col = own_plan.reshape(count, 1)
    orders = [jax.ShapeDtypeStruct((size, count), BF16) for size in home_rows]
    ordered = [jax.ShapeDtypeStruct((size, width), BF16) for size in home_rows]
    even, odd, order_even, order_odd, where_row, where_col = pl.pallas_call(
        functools.partial(order_kernel, bags, pack),
        in_specs=[vmem] * 3,
        out_specs=[vmem] * 6,
        out_shape=ordered + orders + [
            jax.ShapeDtypeStruct((1, count), jnp.int32),
            jax.ShapeDtypeStruct((count, 1), jnp.int32),
        ],
        compiler_params=params(),
        name="order",
    )(plan_col, plan_row, home_tokens)
    full_even = lax.all_gather(even, "bag", axis=1, tiled=True)
    full_odd = lax.all_gather(odd, "bag", axis=1, tiled=True)

    send_even, send_odd, kind_even, kind_odd, final = pl.pallas_call(
        functools.partial(send_kernel, bags, pack, half),
        in_specs=[smem, smem] + [vmem] * 5,
        out_specs=[vmem] * 5,
        out_shape=[jax.ShapeDtypeStruct((slots, size), BF16) for size in home_rows]
        + [jax.ShapeDtypeStruct((size, 128), F32) for size in home_rows]
        + [jax.ShapeDtypeStruct((count, 2 * slots), BF16)],
        compiler_params=params(),
        name="send_plan",
    )(ends, modality, plan_row, where_row, where_col, order_even, order_odd)
    pack_even, pack_odd, back, samples = pl.pallas_call(
        functools.partial(bag_kernel, pack, half),
        in_specs=[smem, smem, vmem],
        out_specs=[vmem] * 4,
        out_shape=[jax.ShapeDtypeStruct((size, slots), BF16) for size in bag_rows]
        + [jax.ShapeDtypeStruct((2 * slots, rows), BF16), jax.ShapeDtypeStruct((rows, 128), F32)],
        scratch_shapes=[pltpu.VMEM((slots, 128), BF16)],
        compiler_params=params(),
        name="bag_plan",
    )(me.reshape(1).astype(jnp.int32), ends, row_plan.reshape(bags, count))
    sample_row = samples[:, 0].reshape(1, rows)

    def to_bag(full, kinds, send, packer):
        outgoing = project(full, kinds, mod_weight, send).reshape(bags, half, width)
        arrived = lax.all_to_all(outgoing, "dp", split_axis=0, concat_axis=0, tiled=True)
        packed = dot(packer, arrived.reshape(slots, width)).astype(BF16)
        return lax.all_gather(packed, "bag", axis=1, tiled=True)

    bag_even = to_bag(full_even, kind_even, send_even, pack_even)
    bag_odd = to_bag(full_odd, kind_odd, send_odd, pack_odd)
    parts_even = make_qkv(bag_even, qkv_weight, norm_gain)
    parts_odd = make_qkv(bag_odd, qkv_weight, norm_gain)
    attended = attend(samples, sample_row, parts_even, parts_odd)
    partial = dot(attended, output_weight).astype(BF16)
    summed = line_sum(partial, width)
    outgoing = dot(back, summed).astype(BF16).reshape(bags, capacity, width)
    returned = lax.all_to_all(outgoing, "dp", split_axis=0, concat_axis=0, tiled=True)
    return dot(final, returned.reshape(bags * capacity, width)).astype(BF16)


def solution(mesh):
    in_specs = (
        P("dp", "bag"),
        P(None, None, "bag"),
        P(None, None, "bag"),
        P(None, "bag"),
        P("bag", None),
        P(),
        P(),
        P(),
    )
    return jax.shard_map(body, mesh=mesh, in_specs=in_specs, out_specs=P("dp", "bag"), check_vma=False)
```

```python
import functools

import jax
import jax.numpy as jnp
from jax import lax
from jax.experimental import pallas as pl
from jax.experimental.pallas import tpu as pltpu
from jax.sharding import PartitionSpec as P

HD = 64
EPSILON = 1e-06
VMEM_LIMIT = 56 * 1024 * 1024
BF16 = jnp.bfloat16
F32 = jnp.float32


def params():
    return pltpu.CompilerParams(vmem_limit_bytes=VMEM_LIMIT)


def up16(count):
    return (count + 15) // 16 * 16


def iota(shape, dim):
    return lax.broadcasted_iota(jnp.int32, shape, dim)


def dot(left, right):
    return jnp.dot(left, right, preferred_element_type=F32)


def dot_nt(left, right):
    return lax.dot_general(left, right, (((1,), (1,)), ((), ())), preferred_element_type=F32)


def total(mask, axis):
    return jnp.sum(jnp.where(mask, 1.0, 0.0), axis=axis, keepdims=True).astype(jnp.int32)


def bag_numbers(plan, bags, pack):
    number = jnp.zeros_like(plan)
    for bag in range(1, bags):
        number += (plan >= bag * pack).astype(jnp.int32)
    return number


def order_kernel(bags, pack, plan_col, plan_row, tokens, even, odd, order_even, order_odd, where_row, where_col):
    count = plan_row.shape[1]
    bag_col = bag_numbers(plan_col[...], bags, pack)
    bag_row = bag_numbers(plan_row[...], bags, pack)
    same = bag_col == bag_row
    above = iota((count, count), 0) < iota((count, count), 1)
    below = iota((count, count), 0) > iota((count, count), 1)
    place_col = total(same & below, 1)
    place_row = total(same & above, 0)
    part_col = place_col & 1
    part_row = place_row & 1
    for part, (ordered, order) in enumerate(((even, order_even), (odd, order_odd))):
        rank_row = total(above & (part_col == part), 0)
        rows = ordered.shape[0]
        onehot = ((iota((rows, count), 0) == rank_row) & (part_row == part)).astype(F32).astype(BF16)
        order[...] = onehot
        ordered[...] = dot(onehot, tokens[...]).astype(BF16)
    where_row[...] = bag_row * 65536 + place_row
    where_col[...] = bag_col * 65536 + place_col


def send_kernel(bags, pack, half, ends, modality, plan_row, where_row, where_col, order_even, order_odd,
                send_even, send_odd, kind_even, kind_odd, final_even, final_odd):
    count = plan_row.shape[1]
    slots = bags * half
    bag_row = where_row[...] >> 16
    place_row = where_row[...] & 65535
    bag_col = where_col[...] >> 16
    place_col = where_col[...] & 65535
    plan = plan_row[...]
    kind = jnp.zeros((1, count), F32)
    for bag in range(bags):
        begin = bag * pack
        for sample in range(ends.shape[1]):
            end = bag * pack + ends[bag, sample]
            inside = (plan >= begin) & (plan < end)
            kind = jnp.where(inside, modality[bag, sample].astype(F32), kind)
            begin = end
    slot_row = bag_row * half + (place_row >> 1)
    for part, (order, send, kinds) in enumerate(((order_even, send_even, kind_even), (order_odd, send_odd, kind_odd))):
        target = (iota((slots, count), 0) == slot_row) & ((place_row & 1) == part)
        send[...] = dot_nt(target.astype(F32).astype(BF16), order[...]).astype(BF16)
        picked = jnp.sum(order[...].astype(F32) * kind, axis=1, keepdims=True)
        kinds[...] = jnp.broadcast_to(picked, kinds.shape)
    slot_col = bag_col * half + (place_col >> 1)
    for part, final in enumerate((final_even, final_odd)):
        match = (iota((count, slots), 1) == slot_col) & ((place_col & 1) == part)
        final[...] = match.astype(F32).astype(BF16)


def bag_kernel(pack, half, me, ends, plan, pack_even, pack_odd, back_even, back_odd, samples, held):
    homes, count = plan.shape
    slot = plan[...] - me[0] * pack
    mine = (slot >= 0) & (slot < pack)
    ahead = (iota((count, count), 0) < iota((count, count), 1)).astype(F32).astype(BF16)
    place = dot(mine.astype(F32).astype(BF16), ahead).astype(jnp.int32)
    place = jnp.where(mine, place, -1)
    filled = total(mine, 1)
    first = 0
    for part, (packer, back) in enumerate(((pack_even, back_even), (pack_odd, back_odd))):
        rows, slots = packer.shape
        lanes = iota((1, slots), 1)
        shift = jnp.zeros((1, slots), jnp.int32)
        limit = jnp.zeros((1, slots), jnp.int32)
        start = jnp.zeros((1, 1), jnp.int32)
        for home in range(homes):
            here = (filled[home:home + 1, :] + (1 - part)) >> 1
            of_home = (lanes >= home * half) & (lanes < (home + 1) * half)
            shift = jnp.where(of_home, start - home * half, shift)
            limit = jnp.where(of_home, here + home * half, limit)
            down = iota((half, back.shape[1]), 0)
            across = iota((half, back.shape[1]), 1)
            block = ((across == down + start) & (down < here)).astype(F32).astype(BF16)
            back[home * half:(home + 1) * half, :] = block
            chosen = place[home:home + 1, :] == iota((half, count), 0) * 2 + part
            slot_here = jnp.sum(jnp.where(chosen, slot[home:home + 1, :].astype(F32), 0.0), axis=1, keepdims=True)
            slot_here = slot_here.astype(jnp.int32)
            number = jnp.ones((half, 1), jnp.int32)
            for sample in range(ends.shape[1]):
                number += (slot_here >= ends[me[0], sample]).astype(jnp.int32)
            held[home * half:(home + 1) * half, :] = jnp.broadcast_to(number.astype(F32), (half, held.shape[1])).astype(BF16)
            start = start + here
        onehot = ((iota((rows, slots), 0) == lanes + shift) & (lanes < limit)).astype(F32).astype(BF16)
        packer[...] = onehot
        samples[first:first + rows, :] = dot(onehot, held[...])
        first += rows


def project_kernel(rows_in, kinds, weight, send, out):
    rows = rows_in[...]
    image = dot(rows, weight[0])
    video = dot(rows, weight[1])
    projected = jnp.where(kinds[:, :1] == 0.0, image, video).astype(BF16)
    out[...] = dot(send[...], projected).astype(BF16)


def project(rows_in, kinds, weight, send):
    rows, depth = rows_in.shape
    width = weight.shape[2]
    step = 256 if width % 256 == 0 else width
    slots = send.shape[0]
    return pl.pallas_call(
        project_kernel,
        grid=(width // step,),
        in_specs=[
            pl.BlockSpec((rows, depth), lambda i: (0, 0)),
            pl.BlockSpec(kinds.shape, lambda i: (0, 0)),
            pl.BlockSpec((2, depth, step), lambda i: (0, 0, i)),
            pl.BlockSpec(send.shape, lambda i: (0, 0)),
        ],
        out_specs=pl.BlockSpec((slots, step), lambda i: (0, i)),
        out_shape=jax.ShapeDtypeStruct((slots, width), BF16),
        compiler_params=params(),
        cost_estimate=pl.CostEstimate(
            flops=4 * rows * depth * width, bytes_accessed=weight.size * 2, transcendentals=0
        ),
        name="project",
    )(rows_in, kinds, weight, send)


def split_dot(value, square):
    high = value.astype(BF16)
    low = (value - high.astype(F32)).astype(BF16)
    return dot(high, square) + dot(low, square)


def qkv_kernel(rows_in, weight, gain, queries, keys, values):
    rows = rows_in[...]
    step = weight.shape[2]
    square = (iota((step, step), 0) // HD == iota((step, step), 1) // HD).astype(F32) * (1.0 / HD)
    square = square.astype(BF16)
    raw_queries = dot(rows, weight[0])
    raw_keys = dot(rows, weight[1])
    values[...] = dot(rows, weight[2]).astype(BF16)
    for index, (raw, out, scale) in enumerate(((raw_queries, queries, HD ** -0.5), (raw_keys, keys, 1.0))):
        shifted = raw - split_dot(raw, square)
        spread = split_dot(shifted * shifted, square)
        out[...] = (shifted * lax.rsqrt(spread + EPSILON) * gain[0, index:index + 1, :] * scale).astype(BF16)


def make_qkv(rows_in, weight, gain):
    rows, depth = rows_in.shape
    width = weight.shape[2]
    step = 256 if width % 256 == 0 else 128
    part = pl.BlockSpec((rows, step), lambda i: (0, i))
    shape = jax.ShapeDtypeStruct((rows, width), BF16)
    return pl.pallas_call(
        qkv_kernel,
        grid=(width // step,),
        in_specs=[
            pl.BlockSpec((rows, depth), lambda i: (0, 0)),
            pl.BlockSpec((3, depth, step), lambda i: (0, 0, i)),
            pl.BlockSpec((1, 2, step), lambda i: (i, 0, 0)),
        ],
        out_specs=[part] * 3,
        out_shape=[shape] * 3,
        compiler_params=params(),
        cost_estimate=pl.CostEstimate(
            flops=6 * rows * depth * width, bytes_accessed=weight.size * 2, transcendentals=0
        ),
        name="qkv",
    )(rows_in, weight, gain.reshape(2, width // step, step).transpose(1, 0, 2))


def attend_kernel(sample_col, sample_row, query, ka, va, kb, vb, out, bias, keys, values):
    first = ka.shape[0]
    count, width = query.shape

    @pl.when(pl.program_id(0) == 0)
    def _():
        bias[...] = jnp.where(sample_col[:, :1] == sample_row[...], 0.0, -1e30)

    keys[:first, :] = ka[...]
    keys[first:, :] = kb[...]
    values[:first, :] = va[...]
    values[first:, :] = vb[...]
    lanes = iota((count, width), 1)
    result = jnp.zeros((count, width), F32)
    for head in range(width // HD):
        own = (lanes >= head * HD) & (lanes < (head + 1) * HD)
        masked = jnp.where(own, query[...], jnp.zeros_like(query))
        scores = dot_nt(masked, keys[...]) + bias[...]
        top = jnp.max(scores, axis=1, keepdims=True)
        raised = jnp.exp(scores - top)
        weight = jnp.sum(raised, axis=1, keepdims=True)
        mixed = dot(raised.astype(BF16), values[...]) / weight
        result = jnp.where(own, mixed, result)
    out[...] = result.astype(BF16)


def attend(sample_col, sample_row, query, parts_a, parts_b):
    count, width = query.shape
    first = parts_a[0].shape[0]
    second = parts_b[0].shape[0]
    rows = first + second
    step = 256 if width % 256 == 0 else 128
    spec_a = pl.BlockSpec((first, step), lambda i: (0, i))
    spec_b = pl.BlockSpec((second, step), lambda i: (0, i))
    return pl.pallas_call(
        attend_kernel,
        grid=(width // step,),
        in_specs=[
            pl.BlockSpec(sample_col.shape, lambda i: (0, 0)),
            pl.BlockSpec(sample_row.shape, lambda i: (0, 0)),
            pl.BlockSpec((count, step), lambda i: (0, i)),
        ] + [spec_a] * 2 + [spec_b] * 2,
        out_specs=pl.BlockSpec((count, step), lambda i: (0, i)),
        out_shape=jax.ShapeDtypeStruct((count, width), BF16),
        scratch_shapes=[
            pltpu.VMEM((count, rows), F32),
            pltpu.VMEM((rows, step), BF16),
            pltpu.VMEM((rows, step), BF16),
        ],
        compiler_params=params(),
        cost_estimate=pl.CostEstimate(
            flops=4 * count * rows * width * 2, bytes_accessed=8 * rows * width, transcendentals=count * rows * width // HD
        ),
        name="attend",
    )(sample_col, sample_row, query, *parts_a, *parts_b)


def line_sum(partial):
    members = lax.axis_size("bag")
    mine = lax.axis_index("bag")

    def piece(index):
        index = jnp.clip(index, 0, members - 1)
        return lax.dynamic_index_in_dim(partial, index, 0, keepdims=False).astype(F32)

    up = down = None
    for step in range(1, members):
        to_up = piece(members - step + mine)
        to_down = piece(mine + step - members)
        if step > 1:
            to_up = to_up + up.astype(F32)
            to_down = to_down + down.astype(F32)
        to_up, to_down = lax.optimization_barrier((to_up.astype(BF16), to_down.astype(BF16)))
        up = lax.ppermute(to_up, "bag", [(i, i + 1) for i in range(step)])
        down = lax.ppermute(to_down, "bag", [(i, i - 1) for i in range(members - step, members)])
        up, down = lax.optimization_barrier((up, down))
    return (piece(mine) + up.astype(F32) + down.astype(F32)).astype(BF16)


def own_columns(weight):
    bags = lax.axis_size("dp")
    members = lax.axis_size("bag")
    me = lax.axis_index("dp")
    depth = weight.shape[0]
    width = weight.shape[1] // members
    share = depth // bags
    part = lax.dynamic_slice_in_dim(weight, me * share, share, 0)
    part = part.reshape(share, members, width).transpose(1, 0, 2)
    part = lax.all_to_all(part, "bag", split_axis=0, concat_axis=0, tiled=True)
    shape = (members,)
    bit = bags // 2
    while bit:
        other = lax.ppermute(part, "dp", [(i, i ^ bit) for i in range(bags)])
        high = (me & bit) != 0
        low_part = jnp.where(high, other, part)
        high_part = jnp.where(high, part, other)
        part = jnp.stack([low_part, high_part], axis=len(shape))
        shape = shape + (2,)
        bit //= 2
    return part.reshape(members * depth, width)


def body(
    home_tokens,
    mod_weight,
    qkv_weight,
    norm_gain,
    output_weight,
    row_plan,
    sample_lengths,
    modality,
):
    bags = lax.axis_size("dp")
    me = lax.axis_index("dp")
    count, width = home_tokens.shape
    pack = count + count // 4
    capacity = 2 * count // bags
    half = capacity // 2
    slots = bags * half
    home_rows = (up16(count // 2 + bags // 2), up16(count // 2))
    bag_rows = (up16(pack // 2 + bags // 2), up16(pack // 2))
    rows = sum(bag_rows)
    vmem = pl.BlockSpec(memory_space=pltpu.VMEM)
    smem = pl.BlockSpec(memory_space=pltpu.SMEM)
    ends = jnp.cumsum(sample_lengths, axis=1)

    own_plan = lax.dynamic_slice_in_dim(row_plan, me * count, count, 0)
    plan_row = own_plan.reshape(1, count)
    plan_col = own_plan.reshape(count, 1)
    orders = [jax.ShapeDtypeStruct((size, count), BF16) for size in home_rows]
    ordered = [jax.ShapeDtypeStruct((size, width), BF16) for size in home_rows]
    even, odd, order_even, order_odd, where_row, where_col = pl.pallas_call(
        functools.partial(order_kernel, bags, pack),
        in_specs=[vmem] * 3,
        out_specs=[vmem] * 6,
        out_shape=ordered + orders + [
            jax.ShapeDtypeStruct((1, count), jnp.int32),
            jax.ShapeDtypeStruct((count, 1), jnp.int32),
        ],
        compiler_params=params(),
        name="order",
    )(plan_col, plan_row, home_tokens)
    early_weight, even = lax.optimization_barrier((output_weight, even))
    full_even = lax.all_gather(even, "bag", axis=1, tiled=True)
    columns = own_columns(early_weight)
    full_odd = lax.all_gather(odd, "bag", axis=1, tiled=True)

    send_even, send_odd, kind_even, kind_odd, final_even, final_odd = pl.pallas_call(
        functools.partial(send_kernel, bags, pack, half),
        in_specs=[smem, smem] + [vmem] * 5,
        out_specs=[vmem] * 6,
        out_shape=[jax.ShapeDtypeStruct((slots, size), BF16) for size in home_rows]
        + [jax.ShapeDtypeStruct((size, 128), F32) for size in home_rows]
        + [jax.ShapeDtypeStruct((count, slots), BF16)] * 2,
        compiler_params=params(),
        name="send_plan",
    )(ends, modality, plan_row, where_row, where_col, order_even, order_odd)
    pack_even, pack_odd, back_even, back_odd, samples = pl.pallas_call(
        functools.partial(bag_kernel, pack, half),
        in_specs=[smem, smem, vmem],
        out_specs=[vmem] * 5,
        out_shape=[jax.ShapeDtypeStruct((size, slots), BF16) for size in bag_rows]
        + [jax.ShapeDtypeStruct((slots, size), BF16) for size in bag_rows]
        + [jax.ShapeDtypeStruct((rows, 128), F32)],
        scratch_shapes=[pltpu.VMEM((slots, 128), BF16)],
        compiler_params=params(),
        name="bag_plan",
    )(me.reshape(1).astype(jnp.int32), ends, row_plan.reshape(bags, count))
    sample_row = samples[:, 0].reshape(1, rows)

    def to_bag(full, kinds, send, packer):
        outgoing = project(full, kinds, mod_weight, send).reshape(bags, half, width)
        arrived = lax.all_to_all(outgoing, "dp", split_axis=0, concat_axis=0, tiled=True)
        packed = dot(packer, arrived.reshape(slots, width)).astype(BF16)
        return lax.all_gather(packed, "bag", axis=1, tiled=True)

    bag_even = to_bag(full_even, kind_even, send_even, pack_even)
    bag_odd = to_bag(full_odd, kind_odd, send_odd, pack_odd)
    parts_even = make_qkv(bag_even, qkv_weight, norm_gain)
    parts_odd = make_qkv(bag_odd, qkv_weight, norm_gain)
    first, second = bag_rows
    attended_even = attend(samples[:first], sample_row, parts_even[0], parts_even[1:], parts_odd[1:])
    gathered = lax.all_gather(attended_even, "bag", axis=1, tiled=True)
    attended_odd = attend(samples[first:], sample_row, parts_odd[0], parts_even[1:], parts_odd[1:])
    members = lax.axis_size("bag")
    partial = jnp.stack(
        [dot(attended_odd, output_weight[:, i * width:(i + 1) * width]).astype(BF16) for i in range(members)]
    )
    summed_odd = line_sum(partial)
    summed_even = dot(gathered, columns).astype(BF16)

    def to_home(summed, back):
        outgoing = dot(back, summed).astype(BF16).reshape(bags, half, width)
        returned = lax.all_to_all(outgoing, "dp", split_axis=0, concat_axis=0, tiled=True)
        return returned.reshape(slots, width)

    home_odd = to_home(summed_odd, back_odd)
    home_even = to_home(summed_even, back_even)
    return (dot(final_even, home_even) + dot(final_odd, home_odd)).astype(BF16)


def solution(mesh):
    in_specs = (
        P("dp", "bag"),
        P(None, None, "bag"),
        P(None, None, "bag"),
        P(None, "bag"),
        P("bag", None),
        P(),
        P(),
        P(),
    )
    return jax.shard_map(body, mesh=mesh, in_specs=in_specs, out_specs=P("dp", "bag"), check_vma=False)
```

```python
import functools

import jax
import jax.numpy as jnp
from jax import lax
from jax.experimental import pallas as pl
from jax.experimental.pallas import tpu as pltpu
from jax.sharding import PartitionSpec as P

HD = 64
EPSILON = 1e-06
PERIOD = 8
FIRST = 5
SMALL_BYTES = 240 * 1024
VMEM_LIMIT = 56 * 1024 * 1024
BF16 = jnp.bfloat16
F32 = jnp.float32


def params():
    return pltpu.CompilerParams(vmem_limit_bytes=VMEM_LIMIT)


def up16(count):
    return (count + 15) // 16 * 16


def iota(shape, dim):
    return lax.broadcasted_iota(jnp.int32, shape, dim)


def dot(left, right):
    return jnp.dot(left, right, preferred_element_type=F32)


def dot_nt(left, right):
    return lax.dot_general(left, right, (((1,), (1,)), ((), ())), preferred_element_type=F32)


def total(mask, axis):
    return jnp.sum(jnp.where(mask, 1.0, 0.0), axis=axis, keepdims=True).astype(jnp.int32)


def part_place(place, part):
    cycle, within = place // PERIOD, place % PERIOD
    if part == 0:
        return jnp.where(within < FIRST, cycle * FIRST + within, -1)
    return jnp.where(within >= FIRST, cycle * (PERIOD - FIRST) + within - FIRST, -1)


def part_sizes(rows, groups):
    spare = groups * FIRST * (PERIOD - FIRST)
    first = up16((rows * FIRST + spare + PERIOD - 1) // PERIOD)
    return first, up16((rows * (PERIOD - FIRST) + PERIOD - 1) // PERIOD)


def bag_numbers(plan, bags, pack):
    number = jnp.zeros_like(plan)
    for bag in range(1, bags):
        number += (plan >= bag * pack).astype(jnp.int32)
    return number


def order_onehot(part, place_row, place_col, rows):
    count = place_row.shape[1]
    above = iota((count, count), 0) < iota((count, count), 1)
    rank_row = total(above & (part_place(place_col, part) >= 0), 0)
    chosen = part_place(place_row, part) >= 0
    return ((iota((rows, count), 0) == rank_row) & chosen).astype(F32).astype(BF16)


def order_kernel(bags, pack, plan_row, tokens, even, odd, order_even, order_odd, where_row, where_col):
    count = plan_row.shape[1]
    diagonal = iota((count, count), 0) == iota((count, count), 1)
    plan_col = jnp.sum(jnp.where(diagonal, plan_row[...].astype(F32), 0.0), axis=1, keepdims=True).astype(jnp.int32)
    bag_col = bag_numbers(plan_col, bags, pack)
    bag_row = bag_numbers(plan_row[...], bags, pack)
    same = bag_col == bag_row
    above = iota((count, count), 0) < iota((count, count), 1)
    below = iota((count, count), 0) > iota((count, count), 1)
    place_col = total(same & below, 1)
    place_row = total(same & above, 0)
    for part, (ordered, order) in enumerate(((even, order_even), (odd, order_odd))):
        onehot = order_onehot(part, place_row, place_col, ordered.shape[0])
        order[...] = onehot
        ordered[...] = dot(onehot, tokens[...]).astype(BF16)
    where_row[...] = bag_row * 65536 + place_row
    where_col[...] = bag_col * 65536 + place_col


def move_kernel(onehot, rows, *refs):
    refs[-1][...] = dot(onehot[...], rows[...]).astype(BF16)


def move_rows(name, onehot, rows, after):
    vmem = pl.BlockSpec(memory_space=pltpu.VMEM)
    return pl.pallas_call(
        move_kernel,
        in_specs=[vmem] * 2 + [pl.BlockSpec(memory_space=pl.ANY)] * len(after),
        out_specs=vmem,
        out_shape=jax.ShapeDtypeStruct((onehot.shape[0], rows.shape[1]), BF16),
        compiler_params=params(),
        name=name,
    )(onehot, rows, *after)


def send_kernel(bags, pack, caps, ends, modality, plan_row, where_row, where_col, order_even, order_odd,
                send_even, send_odd, kind_even, kind_odd, final_even, final_odd):
    count = plan_row.shape[1]
    bag_row = where_row[...] >> 16
    place_row = where_row[...] & 65535
    bag_col = where_col[...] >> 16
    place_col = where_col[...] & 65535
    plan = plan_row[...]
    kind = jnp.zeros((1, count), F32)
    for bag in range(bags):
        begin = bag * pack
        for sample in range(ends.shape[1]):
            end = bag * pack + ends[bag, sample]
            inside = (plan >= begin) & (plan < end)
            kind = jnp.where(inside, modality[bag, sample].astype(F32), kind)
            begin = end
    for part, (order, send, kinds) in enumerate(((order_even, send_even, kind_even), (order_odd, send_odd, kind_odd))):
        own_place = part_place(place_row, part)
        target = (iota((bags * caps[part], count), 0) == bag_row * caps[part] + own_place) & (own_place >= 0)
        send[...] = dot_nt(target.astype(F32).astype(BF16), order[...]).astype(BF16)
        picked = jnp.sum(order[...].astype(F32) * kind, axis=1, keepdims=True)
        kinds[...] = jnp.broadcast_to(picked, kinds.shape)
    for part, final in enumerate((final_even, final_odd)):
        own_place = part_place(place_col, part)
        match = (iota((count, bags * caps[part]), 1) == bag_col * caps[part] + own_place) & (own_place >= 0)
        final[...] = match.astype(F32).astype(BF16)


def bag_kernel(pack, caps, me, ends, plan, pack_even, pack_odd, back_even, back_odd, samples, held):
    homes, count = plan.shape
    slot = plan[...] - me[0] * pack
    mine = (slot >= 0) & (slot < pack)
    ahead = (iota((count, count), 0) < iota((count, count), 1)).astype(F32).astype(BF16)
    place = dot(mine.astype(F32).astype(BF16), ahead).astype(jnp.int32)
    place = jnp.where(mine, place, -PERIOD)
    filled = total(mine, 1)
    first = 0
    for part, (packer, back) in enumerate(((pack_even, back_even), (pack_odd, back_odd))):
        rows, slots = packer.shape
        half = caps[part]
        own_place = part_place(place, part)
        whole = filled // PERIOD * FIRST + jnp.minimum(filled % PERIOD, FIRST)
        heres = whole if part == 0 else filled - whole
        lanes = iota((1, slots), 1)
        shift = jnp.zeros((1, slots), jnp.int32)
        limit = jnp.zeros((1, slots), jnp.int32)
        start = jnp.zeros((1, 1), jnp.int32)
        for home in range(homes):
            here = heres[home:home + 1, :]
            of_home = (lanes >= home * half) & (lanes < (home + 1) * half)
            shift = jnp.where(of_home, start - home * half, shift)
            limit = jnp.where(of_home, here + home * half, limit)
            down = iota((half, back.shape[1]), 0)
            across = iota((half, back.shape[1]), 1)
            block = ((across == down + start) & (down < here)).astype(F32).astype(BF16)
            back[home * half:(home + 1) * half, :] = block
            chosen = own_place[home:home + 1, :] == iota((half, count), 0)
            slot_here = jnp.sum(jnp.where(chosen, slot[home:home + 1, :].astype(F32), 0.0), axis=1, keepdims=True)
            slot_here = slot_here.astype(jnp.int32)
            number = jnp.ones((half, 1), jnp.int32)
            for sample in range(ends.shape[1]):
                number += (slot_here >= ends[me[0], sample]).astype(jnp.int32)
            held[home * half:(home + 1) * half, :] = jnp.broadcast_to(number.astype(F32), (half, held.shape[1])).astype(BF16)
            start = start + here
        onehot = ((iota((rows, slots), 0) == lanes + shift) & (lanes < limit)).astype(F32).astype(BF16)
        packer[...] = onehot
        samples[first:first + rows, :] = dot(onehot, held[:slots, :])
        first += rows


def project_kernel(rows_in, kinds, weight, send, *refs):
    out = refs[-1]
    rows = rows_in[...]
    product = dot(rows, weight[0])
    if weight.shape[0] == 2:
        product = jnp.where(kinds[:, :1] == 0.0, product, dot(rows, weight[1]))
    out[...] = dot(send[...], product.astype(BF16)).astype(BF16)


def project(name, rows_in, kinds, weight, send, after=()):
    rows, depth = rows_in.shape
    width = weight.shape[2]
    step = 256 if width % 256 == 0 else width
    slots = send.shape[0]
    return pl.pallas_call(
        project_kernel,
        grid=(width // step,),
        in_specs=[
            pl.BlockSpec((rows, depth), lambda i: (0, 0)),
            pl.BlockSpec(kinds.shape, lambda i: (0, 0)),
            pl.BlockSpec((weight.shape[0], depth, step), lambda i: (0, 0, i)),
            pl.BlockSpec(send.shape, lambda i: (0, 0)),
        ] + [pl.BlockSpec(memory_space=pl.ANY)] * len(after),
        out_specs=pl.BlockSpec((slots, step), lambda i: (0, i)),
        out_shape=jax.ShapeDtypeStruct((slots, width), BF16),
        compiler_params=params(),
        cost_estimate=pl.CostEstimate(
            flops=2 * rows * weight.size, bytes_accessed=weight.size * 2, transcendentals=0
        ),
        name=name,
    )(rows_in, kinds, weight, send, *after)


def split_dot(value, square):
    high = value.astype(BF16)
    low = (value - high.astype(F32)).astype(BF16)
    return dot(high, square) + dot(low, square)


def qkv_kernel(which, rows_in, gain, *refs):
    weights, outs = refs[:len(which)], refs[-len(which):]
    rows = rows_in[...]
    step = gain.shape[2]
    square = (iota((step, step), 0) // HD == iota((step, step), 1) // HD).astype(F32) * (1.0 / HD)
    square = square.astype(BF16)
    raws = [dot(rows, weight[0]) for weight in weights]
    for index, raw, out in zip(which, raws, outs):
        if index == 2:
            out[...] = raw.astype(BF16)
            continue
        shifted = raw - split_dot(raw, square)
        spread = split_dot(shifted * shifted, square)
        scale = HD ** -0.5 if index == 0 else 1.0
        out[...] = (shifted * lax.rsqrt(spread + EPSILON) * gain[0, index:index + 1, :] * scale).astype(BF16)


def make_qkv(rows_in, weight, gain, which, after=()):
    rows, depth = rows_in.shape
    width = weight.shape[2]
    step = 256 if width % 256 == 0 else 128
    part = pl.BlockSpec((rows, step), lambda i: (0, i))
    shape = jax.ShapeDtypeStruct((rows, width), BF16)
    return pl.pallas_call(
        functools.partial(qkv_kernel, which),
        grid=(width // step,),
        in_specs=[
            pl.BlockSpec((rows, depth), lambda i: (0, 0)),
            pl.BlockSpec((1, 2, step), lambda i: (i, 0, 0)),
        ] + [pl.BlockSpec((1, depth, step), lambda i, index=index: (index, 0, i)) for index in which]
        + [pl.BlockSpec(memory_space=pl.ANY)] * len(after),
        out_specs=[part] * len(which),
        out_shape=[shape] * len(which),
        compiler_params=params(),
        cost_estimate=pl.CostEstimate(
            flops=2 * len(which) * rows * depth * width,
            bytes_accessed=2 * len(which) * depth * width,
            transcendentals=0,
        ),
        name="qkv",
    )(rows_in, gain.reshape(2, width // step, step).transpose(1, 0, 2), *[weight] * len(which), *after)


def attend_kernel(counts, sample_col, sample_row, *refs):
    query_count, key_count = counts
    queries, refs = refs[:query_count], refs[query_count:]
    keys_in, refs = refs[:key_count], refs[key_count:]
    values_in, refs = refs[:key_count], refs[key_count:]
    out, bias, query, keys, values = refs[-5:]

    @pl.when(pl.program_id(0) == 0)
    def _():
        bias[...] = jnp.where(sample_col[:, :1] == sample_row[...], 0.0, -1e30)

    for parts, held in ((queries, query), (keys_in, keys), (values_in, values)):
        at = 0
        for part in parts:
            held[at:at + part.shape[0], :] = part[...]
            at += part.shape[0]
    count, width = query.shape
    lanes = iota((count, width), 1)
    result = jnp.zeros((count, width), F32)
    for head in range(width // HD):
        own = (lanes >= head * HD) & (lanes < (head + 1) * HD)
        masked = jnp.where(own, query[...], jnp.zeros_like(query))
        scores = dot_nt(masked, keys[...]) + bias[...]
        top = jnp.max(scores, axis=1, keepdims=True)
        raised = jnp.exp(scores - top)
        weight = jnp.sum(raised, axis=1, keepdims=True)
        mixed = dot(raised.astype(BF16), values[...]) / weight
        result = jnp.where(own, mixed, result)
    out[...] = result.astype(BF16)


def attend(sample_col, sample_row, queries, keys, values, after=()):
    width = queries[0].shape[1]
    count = sum(part.shape[0] for part in queries)
    rows = sum(part.shape[0] for part in keys)
    step = 256 if width % 256 == 0 else 128
    parts = [*queries, *keys, *values]
    return pl.pallas_call(
        functools.partial(attend_kernel, (len(queries), len(keys))),
        grid=(width // step,),
        in_specs=[
            pl.BlockSpec(sample_col.shape, lambda i: (0, 0)),
            pl.BlockSpec(sample_row.shape, lambda i: (0, 0)),
        ] + [pl.BlockSpec((part.shape[0], step), lambda i: (0, i)) for part in parts]
        + [pl.BlockSpec(memory_space=pl.ANY)] * len(after),
        out_specs=pl.BlockSpec((count, step), lambda i: (0, i)),
        out_shape=jax.ShapeDtypeStruct((count, width), BF16),
        scratch_shapes=[
            pltpu.VMEM((count, rows), F32),
            pltpu.VMEM((count, step), BF16),
            pltpu.VMEM((rows, step), BF16),
            pltpu.VMEM((rows, step), BF16),
        ],
        compiler_params=params(),
        cost_estimate=pl.CostEstimate(
            flops=8 * count * rows * width, bytes_accessed=8 * rows * width, transcendentals=count * rows * width // HD
        ),
        name="attend",
    )(sample_col, sample_row, *parts, *after)


def gather(rows):
    return lax.all_gather(rows, "bag", axis=1, tiled=True)


def small_rows(width):
    return SMALL_BYTES // (2 * width) // 16 * 16


def gather_small(rows):
    count, width = rows.shape
    number = -(-count // small_rows(width))
    step = up16(-(-count // number))
    return jnp.concatenate([gather(rows[at:min(at + step, count)]) for at in range(0, count, step)])


def term_kernel(rows, weight, out):
    out[...] = dot(rows[...], weight[...]).astype(BF16)


def terms(rows, weight):
    count, depth = rows.shape
    width = weight.shape[1]
    step = 512
    return pl.pallas_call(
        term_kernel,
        grid=(width // step,),
        in_specs=[
            pl.BlockSpec((count, depth), lambda i: (0, 0)),
            pl.BlockSpec((depth, step), lambda i: (0, i)),
        ],
        out_specs=pl.BlockSpec((count, step), lambda i: (0, i)),
        out_shape=jax.ShapeDtypeStruct((count, width), BF16),
        compiler_params=params(),
        cost_estimate=pl.CostEstimate(
            flops=2 * count * depth * width, bytes_accessed=2 * depth * width, transcendentals=0
        ),
        name="terms",
    )(rows, weight)


def body(
    home_tokens,
    mod_weight,
    qkv_weight,
    norm_gain,
    output_weight,
    row_plan,
    sample_lengths,
    modality,
):
    bags = lax.axis_size("dp")
    me = lax.axis_index("dp")
    count, width = home_tokens.shape
    pack = count + count // 4
    capacity = 2 * count // bags
    caps = (capacity // PERIOD * FIRST, capacity // PERIOD * (PERIOD - FIRST))
    slots = tuple(bags * cap for cap in caps)
    home_rows = part_sizes(count, bags)
    bag_rows = part_sizes(pack, bags)
    rows = sum(bag_rows)
    vmem = pl.BlockSpec(memory_space=pltpu.VMEM)
    smem = pl.BlockSpec(memory_space=pltpu.SMEM)
    ends = jnp.cumsum(sample_lengths, axis=1)

    own_plan = lax.dynamic_slice_in_dim(row_plan, me * count, count, 0)
    plan_row = own_plan.reshape(1, count)
    even, odd, order_even, order_odd, where_row, where_col = pl.pallas_call(
        functools.partial(order_kernel, bags, pack),
        in_specs=[vmem] * 2,
        out_specs=[vmem] * 6,
        out_shape=[jax.ShapeDtypeStruct((size, width), BF16) for size in home_rows]
        + [jax.ShapeDtypeStruct((size, count), BF16) for size in home_rows]
        + [
            jax.ShapeDtypeStruct((1, count), jnp.int32),
            jax.ShapeDtypeStruct((count, 1), jnp.int32),
        ],
        compiler_params=params(),
        name="order",
    )(plan_row, home_tokens)
    full_even = gather(even)
    full_odd = gather_small(odd)
    send_even, send_odd, kind_even, kind_odd, final_even, final_odd = pl.pallas_call(
        functools.partial(send_kernel, bags, pack, caps),
        in_specs=[smem, smem] + [vmem] * 5,
        out_specs=[vmem] * 6,
        out_shape=[jax.ShapeDtypeStruct(shape, BF16) for shape in zip(slots, home_rows)]
        + [jax.ShapeDtypeStruct((size, 128), F32) for size in home_rows]
        + [jax.ShapeDtypeStruct((count, size), BF16) for size in slots],
        compiler_params=params(),
        name="send_plan",
    )(ends, modality, plan_row, where_row, where_col, order_even, order_odd)
    pack_even, pack_odd, back_even, back_odd, samples = pl.pallas_call(
        functools.partial(bag_kernel, pack, caps),
        in_specs=[smem, smem, vmem],
        out_specs=[vmem] * 5,
        out_shape=[jax.ShapeDtypeStruct(shape, BF16) for shape in zip(bag_rows, slots)]
        + [jax.ShapeDtypeStruct(shape, BF16) for shape in zip(slots, bag_rows)]
        + [jax.ShapeDtypeStruct((rows, 128), F32)],
        scratch_shapes=[pltpu.VMEM((max(slots), 128), BF16)],
        compiler_params=params(),
        name="bag_plan",
    )(me.reshape(1).astype(jnp.int32), ends, row_plan.reshape(bags, count))
    sample_row = samples[:, 0].reshape(1, rows)

    def exchange(outgoing):
        arrived = lax.all_to_all(outgoing.reshape(bags, -1, width), "dp", split_axis=0, concat_axis=0, tiled=True)
        return arrived.reshape(-1, width)

    outgoing_odd = project("project", full_odd, kind_odd, mod_weight, send_odd)
    arrived_odd = exchange(outgoing_odd)
    outgoing_even = project("project", full_even, kind_even, mod_weight, send_even, [outgoing_odd])
    arrived_even = exchange(outgoing_even)
    bag_odd = gather(move_rows("pack", pack_odd, arrived_odd, [outgoing_even]))
    packed_even = move_rows("pack", pack_even, arrived_even, [])
    small = small_rows(width)
    bag_late = gather(packed_even[small:])
    bag_early = gather(packed_even[:small])
    every = (0, 1, 2)
    odd = make_qkv(bag_odd, qkv_weight, norm_gain, every)
    early = make_qkv(bag_early, qkv_weight, norm_gain, every)
    late = make_qkv(bag_late, qkv_weight, norm_gain, every, [odd[0], early[0]])
    keys = early[1], late[1], odd[1]
    values = early[2], late[2], odd[2]
    first = bag_rows[0]
    def to_home(rows, back):
        summed = lax.psum_scatter(terms(rows, output_weight), "bag", scatter_dimension=1, tiled=True)
        return exchange(dot(back, summed).astype(BF16))

    attended_even = attend(samples[:first], sample_row, (early[0], late[0]), keys, values)
    home_even = to_home(attended_even, back_even)
    attended_odd = attend(samples[first:], sample_row, (odd[0],), keys, values, [attended_even])
    home_odd = to_home(attended_odd, back_odd)
    return (dot(final_even, home_even) + dot(final_odd, home_odd)).astype(BF16)


def solution(mesh):
    in_specs = (
        P("dp", "bag"),
        P(None, None, "bag"),
        P(None, None, "bag"),
        P(None, "bag"),
        P("bag", None),
        P(),
        P(),
        P(),
    )
    return jax.shard_map(body, mesh=mesh, in_specs=in_specs, out_specs=P("dp", "bag"), check_vma=False)
```

```python
import functools

import jax
import jax.numpy as jnp
from jax import lax
from jax.experimental import pallas as pl
from jax.experimental.pallas import tpu as pltpu
from jax.sharding import PartitionSpec as P

HD = 64
EPSILON = 1e-06
PERIOD = 8
FIRST = 5
SMALL_BYTES = 240 * 1024
VMEM_LIMIT = 56 * 1024 * 1024
SMALL_LIMIT = 24 * 1024 * 1024
BF16 = jnp.bfloat16
F32 = jnp.float32


def params(limit=VMEM_LIMIT):
    return pltpu.CompilerParams(vmem_limit_bytes=limit)


def up16(count):
    return (count + 15) // 16 * 16


def iota(shape, dim):
    return lax.broadcasted_iota(jnp.int32, shape, dim)


def dot(left, right):
    return jnp.dot(left, right, preferred_element_type=F32)


def dot_nt(left, right):
    return lax.dot_general(left, right, (((1,), (1,)), ((), ())), preferred_element_type=F32)


def total(mask, axis):
    return jnp.sum(jnp.where(mask, 1.0, 0.0), axis=axis, keepdims=True).astype(jnp.int32)


def part_place(place, part):
    cycle, within = place // PERIOD, place % PERIOD
    if part == 0:
        return jnp.where(within < FIRST, cycle * FIRST + within, -1)
    return jnp.where(within >= FIRST, cycle * (PERIOD - FIRST) + within - FIRST, -1)


def part_sizes(rows, groups):
    spare = groups * FIRST * (PERIOD - FIRST)
    first = up16((rows * FIRST + spare + PERIOD - 1) // PERIOD)
    return first, up16((rows * (PERIOD - FIRST) + PERIOD - 1) // PERIOD)


def bag_numbers(plan, bags, pack):
    number = jnp.zeros_like(plan)
    for bag in range(1, bags):
        number += (plan >= bag * pack).astype(jnp.int32)
    return number


def order_onehot(part, place_row, place_col, rows):
    count = place_row.shape[1]
    above = iota((count, count), 0) < iota((count, count), 1)
    rank_row = total(above & (part_place(place_col, part) >= 0), 0)
    chosen = part_place(place_row, part) >= 0
    return ((iota((rows, count), 0) == rank_row) & chosen).astype(F32).astype(BF16)


def order_kernel(bags, pack, plan_row, tokens, order_even, order_odd, where_row, where_col, even, *odds):
    count = plan_row.shape[1]
    diagonal = iota((count, count), 0) == iota((count, count), 1)
    plan_col = jnp.sum(jnp.where(diagonal, plan_row[...].astype(F32), 0.0), axis=1, keepdims=True).astype(jnp.int32)
    bag_col = bag_numbers(plan_col, bags, pack)
    bag_row = bag_numbers(plan_row[...], bags, pack)
    same = bag_col == bag_row
    above = iota((count, count), 0) < iota((count, count), 1)
    below = iota((count, count), 0) > iota((count, count), 1)
    place_col = total(same & below, 1)
    place_row = total(same & above, 0)
    for part, (outs, order) in enumerate((((even,), order_even), (odds, order_odd))):
        onehot = order_onehot(part, place_row, place_col, order.shape[0])
        order[...] = onehot
        ordered = dot(onehot, tokens[...]).astype(BF16)
        at = 0
        for out in outs:
            out[...] = ordered[at:at + out.shape[0], :]
            at += out.shape[0]
    where_row[...] = bag_row * 65536 + place_row
    where_col[...] = bag_col * 65536 + place_col


def move_kernel(number, onehot, rows, *refs):
    moved = dot(onehot[...], rows[...]).astype(BF16)
    at = 0
    for out in refs[-number:]:
        out[...] = moved[at:at + out.shape[0], :]
        at += out.shape[0]


def move_rows(name, onehot, rows, sizes, after=()):
    vmem = pl.BlockSpec(memory_space=pltpu.VMEM)
    return pl.pallas_call(
        functools.partial(move_kernel, len(sizes)),
        in_specs=[vmem] * 2 + [pl.BlockSpec(memory_space=pl.ANY)] * len(after),
        out_specs=[vmem] * len(sizes),
        out_shape=[jax.ShapeDtypeStruct((size, rows.shape[1]), BF16) for size in sizes],
        compiler_params=params(),
        name=name,
    )(onehot, rows, *after)


def send_kernel(bags, pack, caps, lengths, modality, plan_row, where_row, where_col, order_even, order_odd,
                send_even, send_odd, kind_even, kind_odd, final_even, final_odd):
    count = plan_row.shape[1]
    bag_row = where_row[...] >> 16
    place_row = where_row[...] & 65535
    bag_col = where_col[...] >> 16
    place_col = where_col[...] & 65535
    plan = plan_row[...]
    kind = jnp.zeros((1, count), F32)
    for bag in range(bags):
        begin = bag * pack
        for sample in range(lengths.shape[1]):
            end = begin + lengths[bag, sample]
            inside = (plan >= begin) & (plan < end)
            kind = jnp.where(inside, modality[bag, sample].astype(F32), kind)
            begin = end
    for part, (order, send, kinds) in enumerate(((order_even, send_even, kind_even), (order_odd, send_odd, kind_odd))):
        own_place = part_place(place_row, part)
        target = (iota((bags * caps[part], count), 0) == bag_row * caps[part] + own_place) & (own_place >= 0)
        send[...] = dot_nt(target.astype(F32).astype(BF16), order[...]).astype(BF16)
        picked = jnp.sum(order[...].astype(F32) * kind, axis=1, keepdims=True)
        kinds[...] = jnp.broadcast_to(picked, kinds.shape)
    for part, final in enumerate((final_even, final_odd)):
        own_place = part_place(place_col, part)
        match = (iota((count, bags * caps[part]), 1) == bag_col * caps[part] + own_place) & (own_place >= 0)
        final[...] = match.astype(F32).astype(BF16)


def bag_counts(pack, me, plan, part):
    slot = plan[...] - me[0] * pack
    mine = (slot >= 0) & (slot < pack)
    filled = total(mine, 1)
    whole = filled // PERIOD * FIRST + jnp.minimum(filled % PERIOD, FIRST)
    return slot, mine, whole if part == 0 else filled - whole


def pack_plan_kernel(pack, caps, me, plan, pack_even, pack_odd):
    for part, packer in enumerate((pack_even, pack_odd)):
        heres = bag_counts(pack, me, plan, part)[2]
        rows, slots = packer.shape
        lanes = iota((1, slots), 1)
        shift = jnp.zeros((1, slots), jnp.int32)
        limit = jnp.zeros((1, slots), jnp.int32)
        start = jnp.zeros((1, 1), jnp.int32)
        for home in range(plan.shape[0]):
            here = heres[home:home + 1, :]
            base = home * caps[part]
            of_home = (lanes >= base) & (lanes < base + caps[part])
            shift = jnp.where(of_home, start - base, shift)
            limit = jnp.where(of_home, here + base, limit)
            start = start + here
        packer[...] = ((iota((rows, slots), 0) == lanes + shift) & (lanes < limit)).astype(F32).astype(BF16)


def bag_kernel(pack, caps, me, lengths, plan, pack_even, pack_odd, back_even, back_odd, samples, held):
    homes, count = plan.shape
    first = 0
    for part, (packer, back) in enumerate(((pack_even, back_even), (pack_odd, back_odd))):
        slot, mine, heres = bag_counts(pack, me, plan, part)
        ahead = (iota((count, count), 0) < iota((count, count), 1)).astype(F32).astype(BF16)
        place = dot(mine.astype(F32).astype(BF16), ahead).astype(jnp.int32)
        own_place = part_place(jnp.where(mine, place, -PERIOD), part)
        rows, slots = packer.shape
        cap = caps[part]
        start = jnp.zeros((1, 1), jnp.int32)
        for home in range(homes):
            here = heres[home:home + 1, :]
            down = iota((cap, rows), 0)
            block = ((iota((cap, rows), 1) == down + start) & (down < here)).astype(F32).astype(BF16)
            back[home * cap:(home + 1) * cap, :] = block
            chosen = own_place[home:home + 1, :] == iota((cap, count), 0)
            slot_here = jnp.sum(jnp.where(chosen, slot[home:home + 1, :].astype(F32), 0.0), axis=1, keepdims=True)
            slot_here = slot_here.astype(jnp.int32)
            number = jnp.ones((cap, 1), jnp.int32)
            end = 0
            for sample in range(lengths.shape[1]):
                end = end + lengths[me[0], sample]
                number += (slot_here >= end).astype(jnp.int32)
            held[home * cap:(home + 1) * cap, :] = jnp.broadcast_to(number.astype(F32), (cap, held.shape[1])).astype(BF16)
            start = start + here
        samples[first:first + rows, :] = dot(packer[...], held[:slots, :])
        first += rows


def project_kernel(number, kinds, weight, send, *refs):
    out, held = refs[-2:]

    @pl.when(pl.program_id(0) == 0)
    def _():
        at = 0
        for part in refs[:number]:
            held[at:at + part.shape[0], :] = part[...]
            at += part.shape[0]

    rows = held[...]
    product = dot(rows, weight[0])
    if weight.shape[0] == 2:
        product = jnp.where(kinds[:, :1] == 0.0, product, dot(rows, weight[1]))
    out[...] = dot(send[...], product.astype(BF16)).astype(BF16)


def project(name, parts, kinds, weight, send, after=()):
    rows = sum(part.shape[0] for part in parts)
    depth = parts[0].shape[1]
    width = weight.shape[2]
    step = 256 if width % 256 == 0 else width
    slots = send.shape[0]
    return pl.pallas_call(
        functools.partial(project_kernel, len(parts)),
        grid=(width // step,),
        in_specs=[
            pl.BlockSpec(kinds.shape, lambda i: (0, 0)),
            pl.BlockSpec((weight.shape[0], depth, step), lambda i: (0, 0, i)),
            pl.BlockSpec(send.shape, lambda i: (0, 0)),
        ] + [pl.BlockSpec(part.shape, lambda i: (0, 0)) for part in parts] + [pl.BlockSpec(memory_space=pl.ANY)] * len(after),
        out_specs=pl.BlockSpec((slots, step), lambda i: (0, i)),
        out_shape=jax.ShapeDtypeStruct((slots, width), BF16),
        scratch_shapes=[pltpu.VMEM((rows, depth), BF16)],
        compiler_params=params(),
        cost_estimate=pl.CostEstimate(
            flops=2 * rows * weight.size, bytes_accessed=weight.size * 2, transcendentals=0
        ),
        name=name,
    )(kinds, weight, send, *parts, *after)


def split_dot(value, square):
    high = value.astype(BF16)
    low = (value - high.astype(F32)).astype(BF16)
    return dot(high, square) + dot(low, square)


def qkv_kernel(which, rows_in, gain, *refs):
    weights, outs = refs[:len(which)], refs[-len(which):]
    rows = rows_in[...]
    step = gain.shape[2]
    square = (iota((step, step), 0) // HD == iota((step, step), 1) // HD).astype(F32) * (1.0 / HD)
    square = square.astype(BF16)
    raws = [dot(rows, weight[0]) for weight in weights]
    for index, raw, out in zip(which, raws, outs):
        if index == 2:
            out[...] = raw.astype(BF16)
            continue
        shifted = raw - split_dot(raw, square)
        spread = split_dot(shifted * shifted, square)
        scale = HD ** -0.5 if index == 0 else 1.0
        out[...] = (shifted * lax.rsqrt(spread + EPSILON) * gain[0, index:index + 1, :] * scale).astype(BF16)


def make_qkv(rows_in, weight, gain, which, after=()):
    rows, depth = rows_in.shape
    width = weight.shape[2]
    step = 256 if width % 256 == 0 else 128
    part = pl.BlockSpec((rows, step), lambda i: (0, i))
    shape = jax.ShapeDtypeStruct((rows, width), BF16)
    return pl.pallas_call(
        functools.partial(qkv_kernel, which),
        grid=(width // step,),
        in_specs=[
            pl.BlockSpec((rows, depth), lambda i: (0, 0)),
            pl.BlockSpec((1, 2, step), lambda i: (i, 0, 0)),
        ] + [pl.BlockSpec((1, depth, step), lambda i, index=index: (index, 0, i)) for index in which]
        + [pl.BlockSpec(memory_space=pl.ANY)] * len(after),
        out_specs=[part] * len(which),
        out_shape=[shape] * len(which),
        compiler_params=params(),
        cost_estimate=pl.CostEstimate(
            flops=2 * len(which) * rows * depth * width,
            bytes_accessed=2 * len(which) * depth * width,
            transcendentals=0,
        ),
        name="qkv",
    )(rows_in, gain.reshape(2, width // step, step).transpose(1, 0, 2), *[weight] * len(which), *after)


def attend_kernel(counts, sample_col, sample_row, *refs):
    query_count, key_count = counts
    queries, refs = refs[:query_count], refs[query_count:]
    keys_in, refs = refs[:key_count], refs[key_count:]
    values_in, refs = refs[:key_count], refs[key_count:]
    out, bias, query, keys, values = refs[-5:]

    @pl.when(pl.program_id(0) == 0)
    def _():
        bias[...] = jnp.where(sample_col[:, :1] == sample_row[...], 0.0, -1e30)

    for parts, held in ((queries, query), (keys_in, keys), (values_in, values)):
        at = 0
        for part in parts:
            held[at:at + part.shape[0], :] = part[...]
            at += part.shape[0]
    count, width = query.shape
    lanes = iota((count, width), 1)
    result = jnp.zeros((count, width), F32)
    for head in range(width // HD):
        own = (lanes >= head * HD) & (lanes < (head + 1) * HD)
        masked = jnp.where(own, query[...], jnp.zeros_like(query))
        scores = dot_nt(masked, keys[...]) + bias[...]
        top = jnp.max(scores, axis=1, keepdims=True)
        raised = jnp.exp(scores - top)
        weight = jnp.sum(raised, axis=1, keepdims=True)
        mixed = dot(raised.astype(BF16), values[...]) / weight
        result = jnp.where(own, mixed, result)
    out[...] = result.astype(BF16)


def attend(sample_col, sample_row, queries, keys, values, after=()):
    width = queries[0].shape[1]
    count = sum(part.shape[0] for part in queries)
    rows = sum(part.shape[0] for part in keys)
    step = 256 if width % 256 == 0 else 128
    parts = [*queries, *keys, *values]
    return pl.pallas_call(
        functools.partial(attend_kernel, (len(queries), len(keys))),
        grid=(width // step,),
        in_specs=[
            pl.BlockSpec(sample_col.shape, lambda i: (0, 0)),
            pl.BlockSpec(sample_row.shape, lambda i: (0, 0)),
        ] + [pl.BlockSpec((part.shape[0], step), lambda i: (0, i)) for part in parts]
        + [pl.BlockSpec(memory_space=pl.ANY)] * len(after),
        out_specs=pl.BlockSpec((count, step), lambda i: (0, i)),
        out_shape=jax.ShapeDtypeStruct((count, width), BF16),
        scratch_shapes=[
            pltpu.VMEM((count, rows), F32),
            pltpu.VMEM((count, step), BF16),
            pltpu.VMEM((rows, step), BF16),
            pltpu.VMEM((rows, step), BF16),
        ],
        compiler_params=params(),
        cost_estimate=pl.CostEstimate(
            flops=8 * count * rows * width, bytes_accessed=8 * rows * width, transcendentals=count * rows * width // HD
        ),
        name="attend",
    )(sample_col, sample_row, *parts, *after)


def gather(rows):
    return lax.all_gather(rows, "bag", axis=1, tiled=True)


def small_rows(width):
    return SMALL_BYTES // (2 * width) // 16 * 16


def small_pieces(count, width):
    number = -(-count // small_rows(width))
    step = up16(-(-count // number))
    return [min(step, count - at) for at in range(0, count, step)]


def term_kernel(rows, weight, out):
    out[...] = dot(rows[...], weight[...]).astype(BF16)


def terms(rows, weight):
    count, depth = rows.shape
    width = weight.shape[1]
    step = 512
    return pl.pallas_call(
        term_kernel,
        grid=(width // step,),
        in_specs=[
            pl.BlockSpec((count, depth), lambda i: (0, 0)),
            pl.BlockSpec((depth, step), lambda i: (0, i)),
        ],
        out_specs=pl.BlockSpec((count, step), lambda i: (0, i)),
        out_shape=jax.ShapeDtypeStruct((count, width), BF16),
        compiler_params=params(SMALL_LIMIT),
        cost_estimate=pl.CostEstimate(
            flops=2 * count * depth * width, bytes_accessed=2 * depth * width, transcendentals=0
        ),
        name="terms",
    )(rows, weight)


def body(
    home_tokens,
    mod_weight,
    qkv_weight,
    norm_gain,
    output_weight,
    row_plan,
    sample_lengths,
    modality,
):
    bags = lax.axis_size("dp")
    me = lax.axis_index("dp")
    count, width = home_tokens.shape
    pack = count + count // 4
    capacity = 2 * count // bags
    caps = (capacity // PERIOD * FIRST, capacity // PERIOD * (PERIOD - FIRST))
    slots = tuple(bags * cap for cap in caps)
    home_rows = part_sizes(count, bags)
    bag_rows = part_sizes(pack, bags)
    odd_pieces = small_pieces(home_rows[1], width)
    rows = sum(bag_rows)
    vmem = pl.BlockSpec(memory_space=pltpu.VMEM)
    smem = pl.BlockSpec(memory_space=pltpu.SMEM)

    own_plan = lax.dynamic_slice_in_dim(row_plan, me * count, count, 0)
    plan_row = own_plan.reshape(1, count)
    order_even, order_odd, where_row, where_col, even, *odds = pl.pallas_call(
        functools.partial(order_kernel, bags, pack),
        in_specs=[vmem] * 2,
        out_specs=[vmem] * (5 + len(odd_pieces)),
        out_shape=[jax.ShapeDtypeStruct((size, count), BF16) for size in home_rows]
        + [
            jax.ShapeDtypeStruct((1, count), jnp.int32),
            jax.ShapeDtypeStruct((count, 1), jnp.int32),
        ]
        + [jax.ShapeDtypeStruct((size, width), BF16) for size in (home_rows[0], *odd_pieces)],
        compiler_params=params(),
        name="order",
    )(plan_row, home_tokens)
    full_even = gather(even)
    full_odds = [gather(odd) for odd in odds]
    send_even, send_odd, kind_even, kind_odd, final_even, final_odd = pl.pallas_call(
        functools.partial(send_kernel, bags, pack, caps),
        in_specs=[smem, smem] + [vmem] * 5,
        out_specs=[vmem] * 6,
        out_shape=[jax.ShapeDtypeStruct(shape, BF16) for shape in zip(slots, home_rows)]
        + [jax.ShapeDtypeStruct((size, 128), F32) for size in home_rows]
        + [jax.ShapeDtypeStruct((count, size), BF16) for size in slots],
        compiler_params=params(),
        name="send_plan",
    )(sample_lengths, modality, plan_row, where_row, where_col, order_even, order_odd)
    home = me.reshape(1).astype(jnp.int32)
    plan = row_plan.reshape(bags, count)
    pack_even, pack_odd = pl.pallas_call(
        functools.partial(pack_plan_kernel, pack, caps),
        in_specs=[smem, vmem],
        out_specs=[vmem] * 2,
        out_shape=[jax.ShapeDtypeStruct(shape, BF16) for shape in zip(bag_rows, slots)],
        compiler_params=params(),
        name="pack_plan",
    )(home, plan)
    back_even, back_odd, samples = pl.pallas_call(
        functools.partial(bag_kernel, pack, caps),
        in_specs=[smem, smem] + [vmem] * 3,
        out_specs=[vmem] * 3,
        out_shape=[jax.ShapeDtypeStruct(shape, BF16) for shape in zip(slots, bag_rows)]
        + [jax.ShapeDtypeStruct((rows, 128), F32)],
        scratch_shapes=[pltpu.VMEM((max(slots), 128), BF16)],
        compiler_params=params(),
        name="bag_plan",
    )(home, sample_lengths, plan, pack_even, pack_odd)
    sample_row = samples[:, 0].reshape(1, rows)

    def exchange(outgoing):
        arrived = lax.all_to_all(outgoing.reshape(bags, -1, width), "dp", split_axis=0, concat_axis=0, tiled=True)
        return arrived.reshape(-1, width)

    outgoing_odd = project("project", full_odds, kind_odd, mod_weight, send_odd)
    arrived_odd = exchange(outgoing_odd)
    outgoing_even = project("project", [full_even], kind_even, mod_weight, send_even, [outgoing_odd])
    arrived_even = exchange(outgoing_even)
    packed_odd, = move_rows("pack", pack_odd, arrived_odd, bag_rows[1:], [outgoing_even])
    bag_odd = gather(packed_odd)
    small = small_rows(width)
    packed_early, packed_late = move_rows("pack", pack_even, arrived_even, (small, bag_rows[0] - small))
    bag_late = gather(packed_late)
    bag_early = gather(packed_early)
    every = (0, 1, 2)
    odd = make_qkv(bag_odd, qkv_weight, norm_gain, every)
    early = make_qkv(bag_early, qkv_weight, norm_gain, every)
    late = make_qkv(bag_late, qkv_weight, norm_gain, every, [odd[0], early[0]])
    keys = early[1], late[1], odd[1]
    values = early[2], late[2], odd[2]
    first = bag_rows[0]
    def to_home(rows, back):
        summed = lax.psum_scatter(terms(rows, output_weight), "bag", scatter_dimension=1, tiled=True)
        return exchange(dot(back, summed).astype(BF16))

    attended_even = attend(samples[:first], sample_row, (early[0], late[0]), keys, values)
    home_even = to_home(attended_even, back_even)
    attended_odd = attend(samples[first:], sample_row, (odd[0],), keys, values, [attended_even])
    home_odd = to_home(attended_odd, back_odd)
    return (dot(final_even, home_even) + dot(final_odd, home_odd)).astype(BF16)


def solution(mesh):
    in_specs = (
        P("dp", "bag"),
        P(None, None, "bag"),
        P(None, None, "bag"),
        P(None, "bag"),
        P("bag", None),
        P(),
        P(),
        P(),
    )
    return jax.shard_map(body, mesh=mesh, in_specs=in_specs, out_specs=P("dp", "bag"), check_vma=False)
```

```python
import functools

import jax
import jax.numpy as jnp
from jax import lax
from jax.experimental import pallas as pl
from jax.experimental.pallas import tpu as pltpu
from jax.sharding import PartitionSpec as P

HD = 64
EPSILON = 1e-06
PERIOD = 10
FIRST = 7
SMALL_BYTES = 240 * 1024
VMEM_LIMIT = 56 * 1024 * 1024
SMALL_LIMIT = 24 * 1024 * 1024
BF16 = jnp.bfloat16
F32 = jnp.float32


def params(limit=VMEM_LIMIT):
    return pltpu.CompilerParams(vmem_limit_bytes=limit)


def up16(count):
    return (count + 15) // 16 * 16


def iota(shape, dim):
    return lax.broadcasted_iota(jnp.int32, shape, dim)


def dot(left, right):
    return jnp.dot(left, right, preferred_element_type=F32)


def dot_nt(left, right):
    return lax.dot_general(left, right, (((1,), (1,)), ((), ())), preferred_element_type=F32)


def total(mask, axis):
    return jnp.sum(jnp.where(mask, 1.0, 0.0), axis=axis, keepdims=True).astype(jnp.int32)


def part_place(place, part):
    cycle, within = place // PERIOD, place % PERIOD
    if part == 0:
        return jnp.where(within < FIRST, cycle * FIRST + within, -1)
    return jnp.where(within >= FIRST, cycle * (PERIOD - FIRST) + within - FIRST, -1)


def part_sizes(rows, groups):
    spare = groups * FIRST * (PERIOD - FIRST)
    first = up16((rows * FIRST + spare + PERIOD - 1) // PERIOD)
    return first, up16((rows * (PERIOD - FIRST) + PERIOD - 1) // PERIOD)


def bag_numbers(plan, bags, pack):
    number = jnp.zeros_like(plan)
    for bag in range(1, bags):
        number += (plan >= bag * pack).astype(jnp.int32)
    return number


def order_onehot(part, place_row, place_col, rows):
    count = place_row.shape[1]
    above = iota((count, count), 0) < iota((count, count), 1)
    rank_row = total(above & (part_place(place_col, part) >= 0), 0)
    chosen = part_place(place_row, part) >= 0
    return ((iota((rows, count), 0) == rank_row) & chosen).astype(F32).astype(BF16)


def order_kernel(bags, pack, plan_row, tokens, order_even, order_odd, where_row, where_col, even, *odds):
    count = plan_row.shape[1]
    diagonal = iota((count, count), 0) == iota((count, count), 1)
    plan_col = jnp.sum(jnp.where(diagonal, plan_row[...].astype(F32), 0.0), axis=1, keepdims=True).astype(jnp.int32)
    bag_col = bag_numbers(plan_col, bags, pack)
    bag_row = bag_numbers(plan_row[...], bags, pack)
    same = bag_col == bag_row
    above = iota((count, count), 0) < iota((count, count), 1)
    below = iota((count, count), 0) > iota((count, count), 1)
    place_col = total(same & below, 1)
    place_row = total(same & above, 0)
    for part, (outs, order) in enumerate((((even,), order_even), (odds, order_odd))):
        onehot = order_onehot(part, place_row, place_col, order.shape[0])
        order[...] = onehot
        ordered = dot(onehot, tokens[...]).astype(BF16)
        at = 0
        for out in outs:
            out[...] = ordered[at:at + out.shape[0], :]
            at += out.shape[0]
    where_row[...] = bag_row * 65536 + place_row
    where_col[...] = bag_col * 65536 + place_col


def move_kernel(number, onehot, rows, *refs):
    moved = dot(onehot[...], rows[...]).astype(BF16)
    at = 0
    for out in refs[-number:]:
        out[...] = moved[at:at + out.shape[0], :]
        at += out.shape[0]


def move_rows(name, onehot, rows, sizes, after=()):
    vmem = pl.BlockSpec(memory_space=pltpu.VMEM)
    return pl.pallas_call(
        functools.partial(move_kernel, len(sizes)),
        in_specs=[vmem] * 2 + [pl.BlockSpec(memory_space=pl.ANY)] * len(after),
        out_specs=[vmem] * len(sizes),
        out_shape=[jax.ShapeDtypeStruct((size, rows.shape[1]), BF16) for size in sizes],
        compiler_params=params(),
        name=name,
    )(onehot, rows, *after)


def send_kernel(bags, pack, caps, lengths, modality, plan_row, where_row, where_col, order_even, order_odd,
                send_even, send_odd, kind_even, kind_odd, final_even, final_odd):
    count = plan_row.shape[1]
    bag_row = where_row[...] >> 16
    place_row = where_row[...] & 65535
    bag_col = where_col[...] >> 16
    place_col = where_col[...] & 65535
    plan = plan_row[...]
    kind = jnp.zeros((1, count), F32)
    for bag in range(bags):
        begin = bag * pack
        for sample in range(lengths.shape[1]):
            end = begin + lengths[bag, sample]
            inside = (plan >= begin) & (plan < end)
            kind = jnp.where(inside, modality[bag, sample].astype(F32), kind)
            begin = end
    for part, (order, send, kinds) in enumerate(((order_even, send_even, kind_even), (order_odd, send_odd, kind_odd))):
        own_place = part_place(place_row, part)
        target = (iota((bags * caps[part], count), 0) == bag_row * caps[part] + own_place) & (own_place >= 0)
        send[...] = dot_nt(target.astype(F32).astype(BF16), order[...]).astype(BF16)
        picked = jnp.sum(order[...].astype(F32) * kind, axis=1, keepdims=True)
        kinds[...] = jnp.broadcast_to(picked, kinds.shape)
    for part, final in enumerate((final_even, final_odd)):
        own_place = part_place(place_col, part)
        match = (iota((count, bags * caps[part]), 1) == bag_col * caps[part] + own_place) & (own_place >= 0)
        final[...] = match.astype(F32).astype(BF16)


def bag_counts(pack, me, plan, part):
    slot = plan[...] - me[0] * pack
    mine = (slot >= 0) & (slot < pack)
    filled = total(mine, 1)
    whole = filled // PERIOD * FIRST + jnp.minimum(filled % PERIOD, FIRST)
    return slot, mine, whole if part == 0 else filled - whole


def pack_plan_kernel(pack, caps, me, plan, pack_even, pack_odd):
    for part, packer in enumerate((pack_even, pack_odd)):
        heres = bag_counts(pack, me, plan, part)[2]
        rows, slots = packer.shape
        lanes = iota((1, slots), 1)
        shift = jnp.zeros((1, slots), jnp.int32)
        limit = jnp.zeros((1, slots), jnp.int32)
        start = jnp.zeros((1, 1), jnp.int32)
        for home in range(plan.shape[0]):
            here = heres[home:home + 1, :]
            base = home * caps[part]
            of_home = (lanes >= base) & (lanes < base + caps[part])
            shift = jnp.where(of_home, start - base, shift)
            limit = jnp.where(of_home, here + base, limit)
            start = start + here
        packer[...] = ((iota((rows, slots), 0) == lanes + shift) & (lanes < limit)).astype(F32).astype(BF16)


def bag_kernel(pack, caps, me, lengths, plan, pack_even, pack_odd, back_even, back_odd, samples, held):
    homes, count = plan.shape
    first = 0
    for part, (packer, back) in enumerate(((pack_even, back_even), (pack_odd, back_odd))):
        slot, mine, heres = bag_counts(pack, me, plan, part)
        ahead = (iota((count, count), 0) < iota((count, count), 1)).astype(F32).astype(BF16)
        place = dot(mine.astype(F32).astype(BF16), ahead).astype(jnp.int32)
        own_place = part_place(jnp.where(mine, place, -PERIOD), part)
        rows, slots = packer.shape
        cap = caps[part]
        start = jnp.zeros((1, 1), jnp.int32)
        for home in range(homes):
            here = heres[home:home + 1, :]
            down = iota((cap, rows), 0)
            block = ((iota((cap, rows), 1) == down + start) & (down < here)).astype(F32).astype(BF16)
            back[home * cap:(home + 1) * cap, :] = block
            chosen = own_place[home:home + 1, :] == iota((cap, count), 0)
            slot_here = jnp.sum(jnp.where(chosen, slot[home:home + 1, :].astype(F32), 0.0), axis=1, keepdims=True)
            slot_here = slot_here.astype(jnp.int32)
            number = jnp.ones((cap, 1), jnp.int32)
            end = 0
            for sample in range(lengths.shape[1]):
                end = end + lengths[me[0], sample]
                number += (slot_here >= end).astype(jnp.int32)
            held[home * cap:(home + 1) * cap, :] = jnp.broadcast_to(number.astype(F32), (cap, held.shape[1])).astype(BF16)
            start = start + here
        samples[first:first + rows, :] = dot(packer[...], held[:slots, :])
        first += rows


def project_kernel(number, kinds, weight, send, *refs):
    out, held = refs[-2:]

    @pl.when(pl.program_id(0) == 0)
    def _():
        at = 0
        for part in refs[:number]:
            held[at:at + part.shape[0], :] = part[...]
            at += part.shape[0]

    rows = held[...]
    product = dot(rows, weight[0])
    if weight.shape[0] == 2:
        product = jnp.where(kinds[:, :1] == 0.0, product, dot(rows, weight[1]))
    out[...] = dot(send[...], product.astype(BF16)).astype(BF16)


def project(name, parts, kinds, weight, send, after=()):
    rows = sum(part.shape[0] for part in parts)
    depth = parts[0].shape[1]
    width = weight.shape[2]
    step = 256 if width % 256 == 0 else width
    slots = send.shape[0]
    return pl.pallas_call(
        functools.partial(project_kernel, len(parts)),
        grid=(width // step,),
        in_specs=[
            pl.BlockSpec(kinds.shape, lambda i: (0, 0)),
            pl.BlockSpec((weight.shape[0], depth, step), lambda i: (0, 0, i)),
            pl.BlockSpec(send.shape, lambda i: (0, 0)),
        ] + [pl.BlockSpec(part.shape, lambda i: (0, 0)) for part in parts] + [pl.BlockSpec(memory_space=pl.ANY)] * len(after),
        out_specs=pl.BlockSpec((slots, step), lambda i: (0, i)),
        out_shape=jax.ShapeDtypeStruct((slots, width), BF16),
        scratch_shapes=[pltpu.VMEM((rows, depth), BF16)],
        compiler_params=params(SMALL_LIMIT),
        cost_estimate=pl.CostEstimate(
            flops=2 * rows * weight.size, bytes_accessed=weight.size * 2, transcendentals=0
        ),
        name=name,
    )(kinds, weight, send, *parts, *after)


def split_dot(value, square):
    high = value.astype(BF16)
    low = (value - high.astype(F32)).astype(BF16)
    return dot(high, square) + dot(low, square)


def qkv_kernel(which, rows_in, gain, *refs):
    weights, outs = refs[:len(which)], refs[-len(which):]
    rows = rows_in[...]
    step = gain.shape[2]
    square = (iota((step, step), 0) // HD == iota((step, step), 1) // HD).astype(F32) * (1.0 / HD)
    square = square.astype(BF16)
    raws = [dot(rows, weight[0]) for weight in weights]
    for index, raw, out in zip(which, raws, outs):
        if index == 2:
            out[...] = raw.astype(BF16)
            continue
        shifted = raw - split_dot(raw, square)
        spread = split_dot(shifted * shifted, square)
        scale = HD ** -0.5 if index == 0 else 1.0
        out[...] = (shifted * lax.rsqrt(spread + EPSILON) * gain[0, index:index + 1, :] * scale).astype(BF16)


def make_qkv(rows_in, weight, gain, which, after=()):
    rows, depth = rows_in.shape
    width = weight.shape[2]
    step = 256 if width % 256 == 0 else 128
    part = pl.BlockSpec((rows, step), lambda i: (0, i))
    shape = jax.ShapeDtypeStruct((rows, width), BF16)
    return pl.pallas_call(
        functools.partial(qkv_kernel, which),
        grid=(width // step,),
        in_specs=[
            pl.BlockSpec((rows, depth), lambda i: (0, 0)),
            pl.BlockSpec((1, 2, step), lambda i: (i, 0, 0)),
        ] + [pl.BlockSpec((1, depth, step), lambda i, index=index: (index, 0, i)) for index in which]
        + [pl.BlockSpec(memory_space=pl.ANY)] * len(after),
        out_specs=[part] * len(which),
        out_shape=[shape] * len(which),
        compiler_params=params(SMALL_LIMIT),
        cost_estimate=pl.CostEstimate(
            flops=2 * len(which) * rows * depth * width,
            bytes_accessed=2 * len(which) * depth * width,
            transcendentals=0,
        ),
        name="qkv",
    )(rows_in, gain.reshape(2, width // step, step).transpose(1, 0, 2), *[weight] * len(which), *after)


def attend_kernel(counts, sample_col, sample_row, *refs):
    query_count, key_count = counts
    queries, refs = refs[:query_count], refs[query_count:]
    keys_in, refs = refs[:key_count], refs[key_count:]
    values_in, refs = refs[:key_count], refs[key_count:]
    out, bias, query, keys, values = refs[-5:]

    @pl.when(pl.program_id(0) == 0)
    def _():
        bias[...] = jnp.where(sample_col[:, :1] == sample_row[...], 0.0, -1e30)

    for parts, held in ((queries, query), (keys_in, keys), (values_in, values)):
        at = 0
        for part in parts:
            held[at:at + part.shape[0], :] = part[...]
            at += part.shape[0]
    count, width = query.shape
    lanes = iota((count, width), 1)
    result = jnp.zeros((count, width), F32)
    for head in range(width // HD):
        own = (lanes >= head * HD) & (lanes < (head + 1) * HD)
        masked = jnp.where(own, query[...], jnp.zeros_like(query))
        scores = dot_nt(masked, keys[...]) + bias[...]
        top = jnp.max(scores, axis=1, keepdims=True)
        raised = jnp.exp(scores - top)
        weight = jnp.sum(raised, axis=1, keepdims=True)
        mixed = dot(raised.astype(BF16), values[...]) / weight
        result = jnp.where(own, mixed, result)
    out[...] = result.astype(BF16)


def attend(sample_col, sample_row, queries, keys, values, after=()):
    width = queries[0].shape[1]
    count = sum(part.shape[0] for part in queries)
    rows = sum(part.shape[0] for part in keys)
    step = 256 if width % 256 == 0 else 128
    parts = [*queries, *keys, *values]
    return pl.pallas_call(
        functools.partial(attend_kernel, (len(queries), len(keys))),
        grid=(width // step,),
        in_specs=[
            pl.BlockSpec(sample_col.shape, lambda i: (0, 0)),
            pl.BlockSpec(sample_row.shape, lambda i: (0, 0)),
        ] + [pl.BlockSpec((part.shape[0], step), lambda i: (0, i)) for part in parts]
        + [pl.BlockSpec(memory_space=pl.ANY)] * len(after),
        out_specs=pl.BlockSpec((count, step), lambda i: (0, i)),
        out_shape=jax.ShapeDtypeStruct((count, width), BF16),
        scratch_shapes=[
            pltpu.VMEM((count, rows), F32),
            pltpu.VMEM((count, step), BF16),
            pltpu.VMEM((rows, step), BF16),
            pltpu.VMEM((rows, step), BF16),
        ],
        compiler_params=params(),
        cost_estimate=pl.CostEstimate(
            flops=8 * count * rows * width, bytes_accessed=8 * rows * width, transcendentals=count * rows * width // HD
        ),
        name="attend",
    )(sample_col, sample_row, *parts, *after)


def gather(rows):
    return lax.all_gather(rows, "bag", axis=1, tiled=True)


def small_rows(width):
    return SMALL_BYTES // (2 * width) // 16 * 16


def small_pieces(count, width):
    number = -(-count // small_rows(width))
    step = up16(-(-count // number))
    return [min(step, count - at) for at in range(0, count, step)]


def term_kernel(rows, weight, out):
    out[...] = dot(rows[...], weight[...]).astype(BF16)


def terms(rows, weight):
    count, depth = rows.shape
    width = weight.shape[1]
    step = 512
    return pl.pallas_call(
        term_kernel,
        grid=(width // step,),
        in_specs=[
            pl.BlockSpec((count, depth), lambda i: (0, 0)),
            pl.BlockSpec((depth, step), lambda i: (0, i)),
        ],
        out_specs=pl.BlockSpec((count, step), lambda i: (0, i)),
        out_shape=jax.ShapeDtypeStruct((count, width), BF16),
        compiler_params=params(SMALL_LIMIT),
        cost_estimate=pl.CostEstimate(
            flops=2 * count * depth * width, bytes_accessed=2 * depth * width, transcendentals=0
        ),
        name="terms",
    )(rows, weight)


def body(
    home_tokens,
    mod_weight,
    qkv_weight,
    norm_gain,
    output_weight,
    row_plan,
    sample_lengths,
    modality,
):
    bags = lax.axis_size("dp")
    me = lax.axis_index("dp")
    count, width = home_tokens.shape
    pack = count + count // 4
    capacity = 2 * count // bags
    cycles = -(-capacity // PERIOD)
    caps = (up16(cycles * FIRST), up16(cycles * (PERIOD - FIRST)))
    slots = tuple(bags * cap for cap in caps)
    home_rows = part_sizes(count, bags)
    bag_rows = part_sizes(pack, bags)
    odd_pieces = small_pieces(home_rows[1], width)
    rows = sum(bag_rows)
    vmem = pl.BlockSpec(memory_space=pltpu.VMEM)
    smem = pl.BlockSpec(memory_space=pltpu.SMEM)

    own_plan = lax.dynamic_slice_in_dim(row_plan, me * count, count, 0)
    plan_row = own_plan.reshape(1, count)
    order_even, order_odd, where_row, where_col, even, *odds = pl.pallas_call(
        functools.partial(order_kernel, bags, pack),
        in_specs=[vmem] * 2,
        out_specs=[vmem] * (5 + len(odd_pieces)),
        out_shape=[jax.ShapeDtypeStruct((size, count), BF16) for size in home_rows]
        + [
            jax.ShapeDtypeStruct((1, count), jnp.int32),
            jax.ShapeDtypeStruct((count, 1), jnp.int32),
        ]
        + [jax.ShapeDtypeStruct((size, width), BF16) for size in (home_rows[0], *odd_pieces)],
        compiler_params=params(),
        name="order",
    )(plan_row, home_tokens)
    full_even = gather(even)
    full_odds = [gather(odd) for odd in odds]
    send_even, send_odd, kind_even, kind_odd, final_even, final_odd = pl.pallas_call(
        functools.partial(send_kernel, bags, pack, caps),
        in_specs=[smem, smem] + [vmem] * 5,
        out_specs=[vmem] * 6,
        out_shape=[jax.ShapeDtypeStruct(shape, BF16) for shape in zip(slots, home_rows)]
        + [jax.ShapeDtypeStruct((size, 128), F32) for size in home_rows]
        + [jax.ShapeDtypeStruct((count, size), BF16) for size in slots],
        compiler_params=params(),
        name="send_plan",
    )(sample_lengths, modality, plan_row, where_row, where_col, order_even, order_odd)
    home = me.reshape(1).astype(jnp.int32)
    plan = row_plan.reshape(bags, count)
    pack_even, pack_odd = pl.pallas_call(
        functools.partial(pack_plan_kernel, pack, caps),
        in_specs=[smem, vmem],
        out_specs=[vmem] * 2,
        out_shape=[jax.ShapeDtypeStruct(shape, BF16) for shape in zip(bag_rows, slots)],
        compiler_params=params(),
        name="pack_plan",
    )(home, plan)
    back_even, back_odd, samples = pl.pallas_call(
        functools.partial(bag_kernel, pack, caps),
        in_specs=[smem, smem] + [vmem] * 3,
        out_specs=[vmem] * 3,
        out_shape=[jax.ShapeDtypeStruct(shape, BF16) for shape in zip(slots, bag_rows)]
        + [jax.ShapeDtypeStruct((rows, 128), F32)],
        scratch_shapes=[pltpu.VMEM((max(slots), 128), BF16)],
        compiler_params=params(),
        name="bag_plan",
    )(home, sample_lengths, plan, pack_even, pack_odd)
    sample_row = samples[:, 0].reshape(1, rows)

    def exchange(outgoing):
        arrived = lax.all_to_all(outgoing.reshape(bags, -1, width), "dp", split_axis=0, concat_axis=0, tiled=True)
        return arrived.reshape(-1, width)

    outgoing_odd = project("project", full_odds, kind_odd, mod_weight, send_odd)
    arrived_odd = exchange(outgoing_odd)
    outgoing_even = project("project", [full_even], kind_even, mod_weight, send_even, [outgoing_odd])
    arrived_even = exchange(outgoing_even)
    packed_odd, = move_rows("pack", pack_odd, arrived_odd, bag_rows[1:])
    bag_odd = gather(packed_odd)
    small = small_rows(width)
    packed_early, packed_late = move_rows("pack", pack_even, arrived_even, (small, bag_rows[0] - small), [samples])
    bag_late = gather(packed_late)
    bag_early = gather(packed_early)
    every = (0, 1, 2)
    odd = make_qkv(bag_odd, qkv_weight, norm_gain, every, [bag_early])
    early = make_qkv(bag_early, qkv_weight, norm_gain, every)
    late = make_qkv(bag_late, qkv_weight, norm_gain, every, [odd[0], early[0]])
    keys = early[1], late[1], odd[1]
    values = early[2], late[2], odd[2]
    first = bag_rows[0]
    def to_home(rows, back):
        summed = lax.psum_scatter(terms(rows, output_weight), "bag", scatter_dimension=1, tiled=True)
        return exchange(dot(back, summed).astype(BF16))

    attended_even = attend(samples[:first], sample_row, (early[0], late[0]), keys, values)
    home_even = to_home(attended_even, back_even)
    attended_odd = attend(samples[first:], sample_row, (odd[0],), keys, values, [attended_even])
    home_odd = to_home(attended_odd, back_odd)
    return (dot(final_even, home_even) + dot(final_odd, home_odd)).astype(BF16)


def solution(mesh):
    in_specs = (
        P("dp", "bag"),
        P(None, None, "bag"),
        P(None, None, "bag"),
        P(None, "bag"),
        P("bag", None),
        P(),
        P(),
        P(),
    )
    return jax.shard_map(body, mesh=mesh, in_specs=in_specs, out_specs=P("dp", "bag"), check_vma=False)
```

```python
import functools

import jax
import jax.numpy as jnp
from jax import lax
from jax.experimental import pallas as pl
from jax.experimental.pallas import tpu as pltpu
from jax.sharding import PartitionSpec as P

HD = 64
EPSILON = 1e-06
PERIOD = 10
FIRST = 7
SMALL_BYTES = 240 * 1024
VMEM_LIMIT = 56 * 1024 * 1024
SMALL_LIMIT = 24 * 1024 * 1024
BF16 = jnp.bfloat16
F32 = jnp.float32


def params(limit=VMEM_LIMIT):
    return pltpu.CompilerParams(vmem_limit_bytes=limit)


def up16(count):
    return (count + 15) // 16 * 16


def iota(shape, dim):
    return lax.broadcasted_iota(jnp.int32, shape, dim)


def dot(left, right):
    return jnp.dot(left, right, preferred_element_type=F32)


def dot_nt(left, right):
    return lax.dot_general(left, right, (((1,), (1,)), ((), ())), preferred_element_type=F32)


def total(mask, axis):
    return jnp.sum(jnp.where(mask, 1.0, 0.0), axis=axis, keepdims=True).astype(jnp.int32)


def part_place(place, part):
    cycle, within = place // PERIOD, place % PERIOD
    if part == 0:
        return jnp.where(within < FIRST, cycle * FIRST + within, -1)
    return jnp.where(within >= FIRST, cycle * (PERIOD - FIRST) + within - FIRST, -1)


def part_sizes(rows, groups):
    spare = groups * FIRST * (PERIOD - FIRST)
    first = up16((rows * FIRST + spare + PERIOD - 1) // PERIOD)
    return first, up16((rows * (PERIOD - FIRST) + PERIOD - 1) // PERIOD)


def bag_numbers(plan, bags, pack):
    number = jnp.zeros_like(plan)
    for bag in range(1, bags):
        number += (plan >= bag * pack).astype(jnp.int32)
    return number


def order_onehot(part, place_row, place_col, rows):
    count = place_row.shape[1]
    above = iota((count, count), 0) < iota((count, count), 1)
    rank_row = total(above & (part_place(place_col, part) >= 0), 0)
    chosen = part_place(place_row, part) >= 0
    return ((iota((rows, count), 0) == rank_row) & chosen).astype(F32).astype(BF16)


def order_kernel(bags, pack, plan_row, tokens, order_even, order_odd, where_row, where_col, even, *odds):
    count = plan_row.shape[1]
    diagonal = iota((count, count), 0) == iota((count, count), 1)
    plan_col = jnp.sum(jnp.where(diagonal, plan_row[...].astype(F32), 0.0), axis=1, keepdims=True).astype(jnp.int32)
    bag_col = bag_numbers(plan_col, bags, pack)
    bag_row = bag_numbers(plan_row[...], bags, pack)
    same = bag_col == bag_row
    above = iota((count, count), 0) < iota((count, count), 1)
    below = iota((count, count), 0) > iota((count, count), 1)
    place_col = total(same & below, 1)
    place_row = total(same & above, 0)
    for part, (outs, order) in enumerate((((even,), order_even), (odds, order_odd))):
        onehot = order_onehot(part, place_row, place_col, order.shape[0])
        order[...] = onehot
        ordered = dot(onehot, tokens[...]).astype(BF16)
        at = 0
        for out in outs:
            out[...] = ordered[at:at + out.shape[0], :]
            at += out.shape[0]
    where_row[...] = bag_row * 65536 + place_row
    where_col[...] = bag_col * 65536 + place_col


def move_kernel(number, onehot, rows, *refs):
    moved = dot(onehot[...], rows[...]).astype(BF16)
    at = 0
    for out in refs[-number:]:
        out[...] = moved[at:at + out.shape[0], :]
        at += out.shape[0]


def move_rows(name, onehot, rows, sizes, after=()):
    vmem = pl.BlockSpec(memory_space=pltpu.VMEM)
    return pl.pallas_call(
        functools.partial(move_kernel, len(sizes)),
        in_specs=[vmem] * 2 + [pl.BlockSpec(memory_space=pl.ANY)] * len(after),
        out_specs=[vmem] * len(sizes),
        out_shape=[jax.ShapeDtypeStruct((size, rows.shape[1]), BF16) for size in sizes],
        compiler_params=params(),
        name=name,
    )(onehot, rows, *after)


def send_kernel(bags, pack, caps, lengths, modality, plan_row, where_row, where_col, order_even, order_odd,
                send_even, send_odd, kind_even, kind_odd, final_even, final_odd):
    count = plan_row.shape[1]
    bag_row = where_row[...] >> 16
    place_row = where_row[...] & 65535
    bag_col = where_col[...] >> 16
    place_col = where_col[...] & 65535
    plan = plan_row[...]
    kind = jnp.zeros((1, count), F32)
    for bag in range(bags):
        begin = bag * pack
        for sample in range(lengths.shape[1]):
            end = begin + lengths[bag, sample]
            inside = (plan >= begin) & (plan < end)
            kind = jnp.where(inside, modality[bag, sample].astype(F32), kind)
            begin = end
    for part, (order, send, kinds) in enumerate(((order_even, send_even, kind_even), (order_odd, send_odd, kind_odd))):
        own_place = part_place(place_row, part)
        target = (iota((bags * caps[part], count), 0) == bag_row * caps[part] + own_place) & (own_place >= 0)
        send[...] = dot_nt(target.astype(F32).astype(BF16), order[...]).astype(BF16)
        picked = jnp.sum(order[...].astype(F32) * kind, axis=1, keepdims=True)
        kinds[...] = jnp.broadcast_to(picked, kinds.shape)
    for part, final in enumerate((final_even, final_odd)):
        own_place = part_place(place_col, part)
        match = (iota((count, bags * caps[part]), 1) == bag_col * caps[part] + own_place) & (own_place >= 0)
        final[...] = match.astype(F32).astype(BF16)


def bag_counts(pack, me, plan, part):
    slot = plan[...] - me[0] * pack
    mine = (slot >= 0) & (slot < pack)
    filled = total(mine, 1)
    whole = filled // PERIOD * FIRST + jnp.minimum(filled % PERIOD, FIRST)
    return slot, mine, whole if part == 0 else filled - whole


def pack_plan_kernel(pack, caps, me, plan, pack_even, pack_odd):
    for part, packer in enumerate((pack_even, pack_odd)):
        heres = bag_counts(pack, me, plan, part)[2]
        rows, slots = packer.shape
        lanes = iota((1, slots), 1)
        shift = jnp.zeros((1, slots), jnp.int32)
        limit = jnp.zeros((1, slots), jnp.int32)
        start = jnp.zeros((1, 1), jnp.int32)
        for home in range(plan.shape[0]):
            here = heres[home:home + 1, :]
            base = home * caps[part]
            of_home = (lanes >= base) & (lanes < base + caps[part])
            shift = jnp.where(of_home, start - base, shift)
            limit = jnp.where(of_home, here + base, limit)
            start = start + here
        packer[...] = ((iota((rows, slots), 0) == lanes + shift) & (lanes < limit)).astype(F32).astype(BF16)


def bag_kernel(pack, caps, me, lengths, plan, pack_even, pack_odd, back_even, back_odd, samples, held):
    homes, count = plan.shape
    first = 0
    for part, (packer, back) in enumerate(((pack_even, back_even), (pack_odd, back_odd))):
        slot, mine, heres = bag_counts(pack, me, plan, part)
        ahead = (iota((count, count), 0) < iota((count, count), 1)).astype(F32).astype(BF16)
        place = dot(mine.astype(F32).astype(BF16), ahead).astype(jnp.int32)
        own_place = part_place(jnp.where(mine, place, -PERIOD), part)
        rows, slots = packer.shape
        cap = caps[part]
        start = jnp.zeros((1, 1), jnp.int32)
        for home in range(homes):
            here = heres[home:home + 1, :]
            down = iota((cap, rows), 0)
            block = ((iota((cap, rows), 1) == down + start) & (down < here)).astype(F32).astype(BF16)
            back[home * cap:(home + 1) * cap, :] = block
            chosen = own_place[home:home + 1, :] == iota((cap, count), 0)
            slot_here = jnp.sum(jnp.where(chosen, slot[home:home + 1, :].astype(F32), 0.0), axis=1, keepdims=True)
            slot_here = slot_here.astype(jnp.int32)
            number = jnp.ones((cap, 1), jnp.int32)
            end = 0
            for sample in range(lengths.shape[1]):
                end = end + lengths[me[0], sample]
                number += (slot_here >= end).astype(jnp.int32)
            held[home * cap:(home + 1) * cap, :] = jnp.broadcast_to(number.astype(F32), (cap, held.shape[1])).astype(BF16)
            start = start + here
        samples[first:first + rows, :] = dot(packer[...], held[:slots, :])
        first += rows


def project_kernel(number, kinds, weight, send, *refs):
    out, held = refs[-2:]

    @pl.when(pl.program_id(0) == 0)
    def _():
        at = 0
        for part in refs[:number]:
            held[at:at + part.shape[0], :] = part[...]
            at += part.shape[0]

    rows = held[...]
    product = dot(rows, weight[0])
    if weight.shape[0] == 2:
        product = jnp.where(kinds[:, :1] == 0.0, product, dot(rows, weight[1]))
    out[...] = dot(send[...], product.astype(BF16)).astype(BF16)


def project(name, parts, kinds, weight, send, after=()):
    rows = sum(part.shape[0] for part in parts)
    depth = parts[0].shape[1]
    width = weight.shape[2]
    step = 256 if width % 256 == 0 else width
    slots = send.shape[0]
    return pl.pallas_call(
        functools.partial(project_kernel, len(parts)),
        grid=(width // step,),
        in_specs=[
            pl.BlockSpec(kinds.shape, lambda i: (0, 0)),
            pl.BlockSpec((weight.shape[0], depth, step), lambda i: (0, 0, i)),
            pl.BlockSpec(send.shape, lambda i: (0, 0)),
        ] + [pl.BlockSpec(part.shape, lambda i: (0, 0)) for part in parts] + [pl.BlockSpec(memory_space=pl.ANY)] * len(after),
        out_specs=pl.BlockSpec((slots, step), lambda i: (0, i)),
        out_shape=jax.ShapeDtypeStruct((slots, width), BF16),
        scratch_shapes=[pltpu.VMEM((rows, depth), BF16)],
        compiler_params=params(),
        cost_estimate=pl.CostEstimate(
            flops=2 * rows * weight.size, bytes_accessed=weight.size * 2, transcendentals=0
        ),
        name=name,
    )(kinds, weight, send, *parts, *after)


def split_dot(value, square):
    high = value.astype(BF16)
    low = (value - high.astype(F32)).astype(BF16)
    return dot(high, square) + dot(low, square)


def qkv_kernel(which, rows_in, gain, *refs):
    weights, outs = refs[:len(which)], refs[-len(which):]
    rows = rows_in[...]
    step = gain.shape[2]
    square = (iota((step, step), 0) // HD == iota((step, step), 1) // HD).astype(F32) * (1.0 / HD)
    square = square.astype(BF16)
    raws = [dot(rows, weight[0]) for weight in weights]
    for index, raw, out in zip(which, raws, outs):
        if index == 2:
            out[...] = raw.astype(BF16)
            continue
        shifted = raw - split_dot(raw, square)
        spread = split_dot(shifted * shifted, square)
        scale = HD ** -0.5 if index == 0 else 1.0
        out[...] = (shifted * lax.rsqrt(spread + EPSILON) * gain[0, index:index + 1, :] * scale).astype(BF16)


def make_qkv(rows_in, weight, gain, which, after=()):
    rows, depth = rows_in.shape
    width = weight.shape[2]
    step = 256 if width % 256 == 0 else 128
    part = pl.BlockSpec((rows, step), lambda i: (0, i))
    shape = jax.ShapeDtypeStruct((rows, width), BF16)
    return pl.pallas_call(
        functools.partial(qkv_kernel, which),
        grid=(width // step,),
        in_specs=[
            pl.BlockSpec((rows, depth), lambda i: (0, 0)),
            pl.BlockSpec((1, 2, step), lambda i: (i, 0, 0)),
        ] + [pl.BlockSpec((1, depth, step), lambda i, index=index: (index, 0, i)) for index in which]
        + [pl.BlockSpec(memory_space=pl.ANY)] * len(after),
        out_specs=[part] * len(which),
        out_shape=[shape] * len(which),
        compiler_params=params(),
        cost_estimate=pl.CostEstimate(
            flops=2 * len(which) * rows * depth * width,
            bytes_accessed=2 * len(which) * depth * width,
            transcendentals=0,
        ),
        name="qkv",
    )(rows_in, gain.reshape(2, width // step, step).transpose(1, 0, 2), *[weight] * len(which), *after)


def attend_kernel(counts, sample_col, sample_row, *refs):
    query_count, key_count = counts
    queries, refs = refs[:query_count], refs[query_count:]
    keys_in, refs = refs[:key_count], refs[key_count:]
    values_in, refs = refs[:key_count], refs[key_count:]
    out, bias, query, keys, values = refs[-5:]

    @pl.when(pl.program_id(0) == 0)
    def _():
        bias[...] = jnp.where(sample_col[:, :1] == sample_row[...], 0.0, -1e30)

    for parts, held in ((queries, query), (keys_in, keys), (values_in, values)):
        at = 0
        for part in parts:
            held[at:at + part.shape[0], :] = part[...]
            at += part.shape[0]
    count, width = query.shape
    lanes = iota((count, width), 1)
    result = jnp.zeros((count, width), F32)
    for head in range(width // HD):
        own = (lanes >= head * HD) & (lanes < (head + 1) * HD)
        masked = jnp.where(own, query[...], jnp.zeros_like(query))
        scores = dot_nt(masked, keys[...]) + bias[...]
        top = jnp.max(scores, axis=1, keepdims=True)
        raised = jnp.exp(scores - top)
        weight = jnp.sum(raised, axis=1, keepdims=True)
        mixed = dot(raised.astype(BF16), values[...]) / weight
        result = jnp.where(own, mixed, result)
    out[...] = result.astype(BF16)


def attend(sample_col, sample_row, queries, keys, values, after=()):
    width = queries[0].shape[1]
    count = sum(part.shape[0] for part in queries)
    rows = sum(part.shape[0] for part in keys)
    step = 256 if width % 256 == 0 else 128
    parts = [*queries, *keys, *values]
    return pl.pallas_call(
        functools.partial(attend_kernel, (len(queries), len(keys))),
        grid=(width // step,),
        in_specs=[
            pl.BlockSpec(sample_col.shape, lambda i: (0, 0)),
            pl.BlockSpec(sample_row.shape, lambda i: (0, 0)),
        ] + [pl.BlockSpec((part.shape[0], step), lambda i: (0, i)) for part in parts]
        + [pl.BlockSpec(memory_space=pl.ANY)] * len(after),
        out_specs=pl.BlockSpec((count, step), lambda i: (0, i)),
        out_shape=jax.ShapeDtypeStruct((count, width), BF16),
        scratch_shapes=[
            pltpu.VMEM((count, rows), F32),
            pltpu.VMEM((count, step), BF16),
            pltpu.VMEM((rows, step), BF16),
            pltpu.VMEM((rows, step), BF16),
        ],
        compiler_params=params(),
        cost_estimate=pl.CostEstimate(
            flops=8 * count * rows * width, bytes_accessed=8 * rows * width, transcendentals=count * rows * width // HD
        ),
        name="attend",
    )(sample_col, sample_row, *parts, *after)


def gather(rows):
    return lax.all_gather(rows, "bag", axis=1, tiled=True)


def small_rows(width):
    return SMALL_BYTES // (2 * width) // 16 * 16


def small_pieces(count, width):
    number = -(-count // small_rows(width))
    step = up16(-(-count // number))
    return [min(step, count - at) for at in range(0, count, step)]


def term_kernel(rows, weight, out):
    out[...] = dot(rows[...], weight[...]).astype(BF16)


def terms(rows, weight):
    count, depth = rows.shape
    width = weight.shape[1]
    step = 512
    return pl.pallas_call(
        term_kernel,
        grid=(width // step,),
        in_specs=[
            pl.BlockSpec((count, depth), lambda i: (0, 0)),
            pl.BlockSpec((depth, step), lambda i: (0, i)),
        ],
        out_specs=pl.BlockSpec((count, step), lambda i: (0, i)),
        out_shape=jax.ShapeDtypeStruct((count, width), BF16),
        compiler_params=params(SMALL_LIMIT),
        cost_estimate=pl.CostEstimate(
            flops=2 * count * depth * width, bytes_accessed=2 * depth * width, transcendentals=0
        ),
        name="terms",
    )(rows, weight)


def body(
    home_tokens,
    mod_weight,
    qkv_weight,
    norm_gain,
    output_weight,
    row_plan,
    sample_lengths,
    modality,
):
    bags = lax.axis_size("dp")
    me = lax.axis_index("dp")
    count, width = home_tokens.shape
    pack = count + count // 4
    capacity = 2 * count // bags
    cycles = -(-capacity // PERIOD)
    caps = (up16(cycles * FIRST), up16(cycles * (PERIOD - FIRST)))
    slots = tuple(bags * cap for cap in caps)
    home_rows = part_sizes(count, bags)
    bag_rows = part_sizes(pack, bags)
    odd_pieces = small_pieces(home_rows[1], width)
    rows = sum(bag_rows)
    vmem = pl.BlockSpec(memory_space=pltpu.VMEM)
    smem = pl.BlockSpec(memory_space=pltpu.SMEM)

    own_plan = lax.dynamic_slice_in_dim(row_plan, me * count, count, 0)
    plan_row = own_plan.reshape(1, count)
    order_even, order_odd, where_row, where_col, even, *odds = pl.pallas_call(
        functools.partial(order_kernel, bags, pack),
        in_specs=[vmem] * 2,
        out_specs=[vmem] * (5 + len(odd_pieces)),
        out_shape=[jax.ShapeDtypeStruct((size, count), BF16) for size in home_rows]
        + [
            jax.ShapeDtypeStruct((1, count), jnp.int32),
            jax.ShapeDtypeStruct((count, 1), jnp.int32),
        ]
        + [jax.ShapeDtypeStruct((size, width), BF16) for size in (home_rows[0], *odd_pieces)],
        compiler_params=params(),
        name="order",
    )(plan_row, home_tokens)
    full_even = gather(even)
    full_odds = [gather(odd) for odd in odds]
    send_even, send_odd, kind_even, kind_odd, final_even, final_odd = pl.pallas_call(
        functools.partial(send_kernel, bags, pack, caps),
        in_specs=[smem, smem] + [vmem] * 5,
        out_specs=[vmem] * 6,
        out_shape=[jax.ShapeDtypeStruct(shape, BF16) for shape in zip(slots, home_rows)]
        + [jax.ShapeDtypeStruct((size, 128), F32) for size in home_rows]
        + [jax.ShapeDtypeStruct((count, size), BF16) for size in slots],
        compiler_params=params(),
        name="send_plan",
    )(sample_lengths, modality, plan_row, where_row, where_col, order_even, order_odd)
    home = me.reshape(1).astype(jnp.int32)
    plan = row_plan.reshape(bags, count)
    pack_even, pack_odd = pl.pallas_call(
        functools.partial(pack_plan_kernel, pack, caps),
        in_specs=[smem, vmem],
        out_specs=[vmem] * 2,
        out_shape=[jax.ShapeDtypeStruct(shape, BF16) for shape in zip(bag_rows, slots)],
        compiler_params=params(),
        name="pack_plan",
    )(home, plan)
    back_even, back_odd, samples = pl.pallas_call(
        functools.partial(bag_kernel, pack, caps),
        in_specs=[smem, smem] + [vmem] * 3,
        out_specs=[vmem] * 3,
        out_shape=[jax.ShapeDtypeStruct(shape, BF16) for shape in zip(slots, bag_rows)]
        + [jax.ShapeDtypeStruct((rows, 128), F32)],
        scratch_shapes=[pltpu.VMEM((max(slots), 128), BF16)],
        compiler_params=params(),
        name="bag_plan",
    )(home, sample_lengths, plan, pack_even, pack_odd)
    sample_row = samples[:, 0].reshape(1, rows)

    def exchange(outgoing):
        arrived = lax.all_to_all(outgoing.reshape(bags, -1, width), "dp", split_axis=0, concat_axis=0, tiled=True)
        return arrived.reshape(-1, width)

    outgoing_odd = project("project", full_odds, kind_odd, mod_weight, send_odd)
    arrived_odd = exchange(outgoing_odd)
    outgoing_even = project("project", [full_even], kind_even, mod_weight, send_even, [outgoing_odd])
    arrived_even = exchange(outgoing_even)
    packed_odd, = move_rows("pack", pack_odd, arrived_odd, bag_rows[1:])
    bag_odd = gather(packed_odd)
    small = small_rows(width)
    packed_early, packed_late = move_rows("pack", pack_even, arrived_even, (small, bag_rows[0] - small), [samples])
    bag_late = gather(packed_late)
    bag_early = gather(packed_early)
    every = (0, 1, 2)
    odd = make_qkv(bag_odd, qkv_weight, norm_gain, every, [bag_early])
    early = make_qkv(bag_early, qkv_weight, norm_gain, every)
    late = make_qkv(bag_late, qkv_weight, norm_gain, every, [odd[0], early[0]])
    keys = early[1], late[1], odd[1]
    values = early[2], late[2], odd[2]
    first = bag_rows[0]
    def to_home(rows, back):
        summed = lax.psum_scatter(terms(rows, output_weight), "bag", scatter_dimension=1, tiled=True)
        return exchange(dot(back, summed).astype(BF16))

    attended_even = attend(samples[:first], sample_row, (early[0], late[0]), keys, values)
    home_even = to_home(attended_even, back_even)
    attended_odd = attend(samples[first:], sample_row, (odd[0],), keys, values, [attended_even])
    home_odd = to_home(attended_odd, back_odd)
    return (dot(final_even, home_even) + dot(final_odd, home_odd)).astype(BF16)


def solution(mesh):
    in_specs = (
        P("dp", "bag"),
        P(None, None, "bag"),
        P(None, None, "bag"),
        P(None, "bag"),
        P("bag", None),
        P(),
        P(),
        P(),
    )
    return jax.shard_map(body, mesh=mesh, in_specs=in_specs, out_specs=P("dp", "bag"), check_vma=False)
```
